32 devices in a mesh: dp: 2 (over core), mp: 16 (over z, y, x).
Axes of the slice: x: 2, y: 2, z: 4, core: 2. Of those that a mesh axis runs over, the one named last changes fastest.
Arguments:
- inputs: bfloat16 [2, 8192, 8192], P('dp', 'mp'), may hold values from -6 to 6
- cotangent: bfloat16 [2, 8192, 8192], P('dp', 'mp'), may hold values from -6 to 6
- mixer_right: bfloat16 [64, 128, 128], replicated, may hold values from -0.5 to 0.5
- mixer_left: bfloat16 [64, 128, 128], replicated, may hold values from -0.5 to 0.5
- dense_right: bfloat16 [64, 128, 128], P('mp'), may hold values from -0.5 to 0.5
- dense_left: bfloat16 [64, 128, 128], P('mp'), may hold values from -0.5 to 0.5
Outputs:
- block_out: bfloat16 [2, 8192, 8192], P('dp', 'mp')
- grad_inputs: bfloat16 [2, 8192, 8192], P('dp', 'mp')
- grad_mixer_right: float32 [64, 128, 128], P('mp', 'dp')
- grad_mixer_left: float32 [64, 128, 128], P('mp', 'dp')
- grad_dense_right: float32 [64, 128, 128], P('mp', 'dp')
- grad_dense_left: float32 [64, 128, 128], P('mp', 'dp')
The draws below stay inside these ranges and needn't reach their ends.
All inputs are finite; a program needn't handle non-finite values.
Results may differ from the reference program's by a relative error of at most 0.015.
Values may be sent and summed in bfloat16 or wider, within the bound.
No kernel may reach another device: no remote copies, remote signals or barrier semaphores. Data moves between devices by JAX's collectives and lax.ppermute only.
A program may use at most 256 MiB of HBM per device.

```python
import jax
import jax.numpy as jnp
from jax import lax

NB = 64
BS = 128
LB = 64
LS = 128
D = 8192
L = 8192
BATCH = 2


def level_of(rng, dims, cuts, least, largest):
    def one(position, parts):
        heights = jax.random.uniform(jax.random.fold_in(jax.random.fold_in(rng, 6), position), (parts,), jnp.float32, least / len(cuts), largest / len(cuts))
        return jnp.repeat(jnp.exp(heights), dims[position] // parts).reshape((-1,) + (1,) * (len(dims) - position - 1))

    loudness = one(*cuts[0])
    for cut in cuts[1:]:
        loudness = loudness * one(*cut)
    return loudness


def noise(key, extent, scale, bound, pieces=(), kind=jnp.bfloat16):
    values = jax.random.normal(key, extent, jnp.float32) * scale
    if len(pieces) > 0:
        values = level_of(key, extent, pieces, -0.22, 0.18) * values
    return jnp.clip(values, min=-bound, max=bound).astype(kind)


def setup_inputs(seed: int = 0) -> dict:
    keys = jax.random.split(jax.random.key(seed), 7)
    return {
        "inputs": noise(keys[0], (BATCH, D, L), 1.0, 6.0, ((0, 2), (1, 16))),
        "cotangent": noise(keys[1], (BATCH, D, L), 1.0, 6.0, ((0, 2), (1, 16))),
        "mixer_right": noise(keys[2], (LB, LS, LS), LS ** -0.5, 0.5),
        "mixer_left": noise(keys[3], (LB, LS, LS), LS ** -0.5, 0.5),
        "dense_right": noise(keys[4], (NB, BS, BS), BS ** -0.5, 0.5, ((0, 16),)),
        "dense_left": noise(keys[5], (NB, BS, BS), BS ** -0.5, 0.5, ((0, 16),)),
    }


HIGH = lax.Precision.HIGHEST


def along_last(values, weight, blocks):
    lead = values.shape[:-1]
    total = values.shape[-1]
    size = total // blocks
    fold = size // blocks
    shaped = values.astype(jnp.float32).reshape(lead + (blocks, size))
    table = weight.astype(jnp.float32).reshape(blocks, size, blocks, fold)
    mixed = jnp.einsum("...bi,bief->...ebf", shaped, table, precision=HIGH)
    return mixed.reshape(lead + (total,))


def back_last(grads, weight, blocks):
    lead = grads.shape[:-1]
    total = grads.shape[-1]
    size = total // blocks
    fold = size // blocks
    shaped = grads.astype(jnp.float32).reshape(lead + (blocks, blocks, fold))
    table = weight.astype(jnp.float32).reshape(blocks, size, blocks, fold)
    result = jnp.einsum("ekbf,...bef->...ek", table, shaped, precision=HIGH)
    return result.reshape(lead + (total,))


def grad_last(values, grads, blocks):
    lead = values.shape[:-1]
    total = values.shape[-1]
    size = total // blocks
    fold = size // blocks
    left_side = values.astype(jnp.float32).reshape(lead + (blocks, size))
    right_side = grads.astype(jnp.float32).reshape(lead + (blocks, blocks, fold))
    result = jnp.einsum("...ek,...bef->ekbf", left_side, right_side, precision=HIGH)
    return result.reshape(blocks, size, size)


def along_first(values, weight, blocks):
    total, length = values.shape
    size = total // blocks
    fold = size // blocks
    shaped = values.astype(jnp.float32).reshape(blocks, size, length)
    table = weight.astype(jnp.float32).reshape(blocks, size, blocks, fold)
    mixed = jnp.einsum("bil,bief->ebfl", shaped, table, precision=HIGH)
    return mixed.reshape(total, length)


def back_first(grads, weight, blocks):
    total, length = grads.shape
    size = total // blocks
    fold = size // blocks
    shaped = grads.astype(jnp.float32).reshape(blocks, blocks, fold, length)
    table = weight.astype(jnp.float32).reshape(blocks, size, blocks, fold)
    result = jnp.einsum("ekbf,befl->ekl", table, shaped, precision=HIGH)
    return result.reshape(total, length)


def grad_first(values, grads, blocks):
    total, length = values.shape
    size = total // blocks
    fold = size // blocks
    left_side = values.astype(jnp.float32).reshape(blocks, size, length)
    right_side = grads.astype(jnp.float32).reshape(blocks, blocks, fold, length)
    result = jnp.einsum("ekl,befl->ekbf", left_side, right_side, precision=HIGH)
    return result.reshape(blocks, size, size)


def reference(inputs, cotangent, mixer_right, mixer_left, dense_right, dense_left):
    def one_sequence(carry, pair):
        source, upstream = pair
        values = source.astype(jnp.float32)
        above = upstream.astype(jnp.float32)
        first_mix = along_last(source, mixer_right, LB).astype(jnp.bfloat16)
        time_mixed = along_last(first_mix, mixer_left, LB).astype(jnp.bfloat16)
        sigma_in = jax.nn.sigmoid(values)
        silu_in = values * sigma_in
        slope_in = sigma_in * (1.0 + values * (1.0 - sigma_in))
        hidden = (values + silu_in * time_mixed.astype(jnp.float32)).astype(jnp.bfloat16)
        hidden_f = hidden.astype(jnp.float32)
        panel = along_first(hidden, dense_right, NB).astype(jnp.bfloat16)
        gate = along_first(panel, dense_left, NB).astype(jnp.bfloat16)
        gate_f = gate.astype(jnp.float32)
        sigma_gate = jax.nn.sigmoid(gate_f)
        silu_gate = gate_f * sigma_gate
        slope_gate = sigma_gate * (1.0 + gate_f * (1.0 - sigma_gate))
        block_out = (hidden_f * (1.0 + silu_gate)).astype(jnp.bfloat16)
        grad_gate = (above * hidden_f * slope_gate).astype(jnp.bfloat16)
        grad_panel = back_first(grad_gate, dense_left, NB).astype(jnp.bfloat16)
        term_dense_left = grad_first(panel, grad_gate, NB)
        grad_hidden = (above * (1.0 + silu_gate) + back_first(grad_panel, dense_right, NB)).astype(jnp.bfloat16)
        term_dense_right = grad_first(hidden, grad_panel, NB)
        grad_hidden_f = grad_hidden.astype(jnp.float32)
        grad_time = (grad_hidden_f * silu_in).astype(jnp.bfloat16)
        grad_first_mix = back_last(grad_time, mixer_left, LB).astype(jnp.bfloat16)
        term_mixer_left = grad_last(first_mix, grad_time, LB)
        grad_inputs = (grad_hidden_f * (1.0 + slope_in * time_mixed.astype(jnp.float32)) + back_last(grad_first_mix, mixer_right, LB)).astype(jnp.bfloat16)
        term_mixer_right = grad_last(source, grad_first_mix, LB)
        carry = (carry[0] + term_mixer_right, carry[1] + term_mixer_left, carry[2] + term_dense_right, carry[3] + term_dense_left)
        return carry, (block_out, grad_inputs)

    empty_mixer = jnp.zeros((LB, LS, LS), jnp.float32)
    empty_dense = jnp.zeros((NB, BS, BS), jnp.float32)
    totals, (block_out, grad_inputs) = lax.scan(one_sequence, (empty_mixer, empty_mixer, empty_dense, empty_dense), (inputs, cotangent))
    dense_scale = float(BATCH * L) ** -0.5
    mixer_scale = float(BATCH * D) ** -0.5
    return (block_out, grad_inputs, totals[0] * mixer_scale, totals[1] * mixer_scale, totals[2] * dense_scale, totals[3] * dense_scale)
```

```python
import functools

import jax
import jax.numpy as jnp
from jax import lax
from jax.experimental import pallas as pl
from jax.experimental.pallas import tpu as pltpu
from jax.sharding import PartitionSpec as P

NB = 64
BS = 128
LB = 64
LS = 128
LANES = 128
CHUNKS = 2
UNROLL = 4
VMEM = 60 * 1024 * 1024
F32 = jnp.float32
BF16 = jnp.bfloat16

NN = (((1,), (0,)), ((), ()))
NT = (((1,), (1,)), ((), ()))
TN = (((0,), (0,)), ((), ()))


def dot(left, right, dims=NN):
    return lax.dot_general(left, right, dims, preferred_element_type=F32)


def each(count, step, unroll=UNROLL):
    def group(index, carry):
        for inner in range(unroll):
            step(index * unroll + inner, inner)
        return carry

    lax.fori_loop(0, count // unroll, group, 0)


def block_of(index, size):
    return pl.ds(pl.multiple_of(index * size, size), size)


def gathered(ref, index, blocks, size):
    fold = size // blocks
    parts = [ref[pl.ds(f * blocks + index, blocks, stride=size), :] for f in range(fold)]
    return jnp.concatenate(parts, 0).astype(BF16)


def gathered_natural(ref, index, blocks, size):
    fold = size // blocks
    parts = [ref[pl.ds(index * fold + f, blocks, stride=size), :] for f in range(fold)]
    return jnp.concatenate(parts, 0).astype(BF16)


def mix_kernel(x_ref, right_ref, left_ref, order_ref, *refs):
    hidden_refs, (time_ref, first_ref, one, two) = refs[:CHUNKS], refs[CHUNKS:]

    def first(b, _):
        one[block_of(b, LS), :] = dot(right_ref[b], x_ref[:, block_of(b, LS)], NT)

    def second(e, _):
        rows = gathered(one, e, LB, LS)
        first_ref[e] = rows
        two[block_of(e, LS), :] = dot(left_ref[e], rows)

    devices, _, piece = hidden_refs[0].shape
    per_device = LB // devices
    per_chunk = piece // LS

    def third(e, inner):
        mixed = dot(gathered(two, e, LB, LS), order_ref[...], TN)
        time_ref[:, block_of(e, LS)] = mixed.astype(BF16)
        x = x_ref[:, block_of(e, LS)].astype(F32)
        hidden = x + x * jax.nn.sigmoid(x) * mixed.astype(BF16).astype(F32)
        place = pl.ds(inner % per_chunk * LS, LS)
        hidden_refs[inner // per_chunk][e // per_device, :, place] = hidden.astype(BF16)

    each(LB, first)
    each(LB, second)
    each(LB, third, per_device)


def feature_kernel(
    hidden_ref, above_ref, right_ref, right_back_ref, left_ref, left_back_ref, order_ref,
    out_ref, grad_ref, term_right_ref, term_left_ref, one, two, direct, panel,
):
    @pl.when(pl.program_id(0) == 0)
    def _():
        term_right_ref[...] = jnp.zeros_like(term_right_ref)
        term_left_ref[...] = jnp.zeros_like(term_left_ref)

    def first(b, _):
        one[block_of(b, BS), :] = dot(right_ref[b], hidden_ref[block_of(b, BS), :])

    def second(e, _):
        rows = gathered(one, e, NB, BS)
        panel[e] = rows
        two[block_of(e, BS), :] = dot(left_ref[e], rows)

    def third(e, _):
        rows = block_of(e, BS)
        gate = dot(order_ref[...], gathered(two, e, NB, BS))
        hidden = hidden_ref[rows, :].astype(F32)
        above = above_ref[rows, :].astype(F32)
        sigma = jax.nn.sigmoid(gate)
        through = 1.0 + gate * sigma
        slope = sigma * (1.0 + gate * (1.0 - sigma))
        out_ref[rows, :] = (hidden * through).astype(BF16)
        direct[rows, :] = above * through
        one[rows, :] = above * hidden * slope

    def fourth(e, _):
        rows = gathered_natural(one, e, NB, BS)
        two[block_of(e, BS), :] = dot(left_back_ref[e], rows)
        term_left_ref[e] += dot(panel[e], rows, NT)

    def fifth(b, _):
        rows = gathered(two, b, NB, BS)
        place = block_of(b, BS)
        grad_ref[place, :] = (direct[place, :] + dot(right_back_ref[b], rows)).astype(BF16)
        term_right_ref[b] += dot(hidden_ref[place, :], rows, NT)

    each(NB, first)
    each(NB, second)
    each(NB, third)
    each(NB, fourth)
    each(NB, fifth)


def back_kernel(x_ref, time_ref, first_ref, right_ref, left_back_ref, eye_ref, *refs):
    grad_refs = refs[:CHUNKS]
    out_ref, term_right_ref, term_left_ref, one, two = refs[CHUNKS:]
    devices, _, piece = grad_refs[0].shape
    per_device = LB // devices
    per_chunk = piece // LS

    @pl.when(pl.program_id(0) == 0)
    def _():
        term_right_ref[...] = jnp.zeros_like(term_right_ref)
        term_left_ref[...] = jnp.zeros_like(term_left_ref)

    def grad_of(e, inner):
        place = pl.ds(inner % per_chunk * LS, LS)
        return grad_refs[inner // per_chunk][e // per_device, :, place].astype(F32)

    def first(e, inner):
        x = x_ref[:, block_of(e, LS)].astype(F32)
        grad_time = (grad_of(e, inner) * (x * jax.nn.sigmoid(x))).astype(BF16)
        one[block_of(e, LS), :] = dot(eye_ref[...], grad_time, NT)

    def second(e, _):
        rows = gathered_natural(one, e, LB, LS)
        two[block_of(e, LS), :] = dot(left_back_ref[e], rows)
        term_left_ref[e] += dot(first_ref[e], rows, NT)

    def third(b, inner):
        place = block_of(b, LS)
        rows = gathered(two, b, LB, LS)
        x = x_ref[:, place]
        term = dot(rows, right_ref[b], TN)
        values = x.astype(F32)
        sigma = jax.nn.sigmoid(values)
        slope = sigma * (1.0 + values * (1.0 - sigma))
        grad = grad_of(b, inner)
        result = grad * (1.0 + slope * time_ref[:, place].astype(F32)) + term
        out_ref[:, place] = result.astype(BF16)
        term_right_ref[b] += lax.dot_general(
            x, rows, (((0,), (1,)), ((), ())), preferred_element_type=F32
        )

    each(LB, first, per_device)
    each(LB, second)
    each(LB, third, per_device)


def split_kernel(whole_ref, *part_refs):
    piece = part_refs[0].shape[-1]
    for part, ref in enumerate(part_refs):
        ref[0] = whole_ref[:, part * piece : (part + 1) * piece]


def join_kernel(*refs):
    whole_ref = refs[-1]
    piece = refs[0].shape[-1]
    for part, ref in enumerate(refs[:-1]):
        whole_ref[:, part * piece : (part + 1) * piece] = ref[0]


def call(kernel, *args, **more):
    return pl.pallas_call(
        kernel, *args, compiler_params=pltpu.CompilerParams(vmem_limit_bytes=VMEM), **more
    )


def fixed(shape):
    return pl.BlockSpec(shape, lambda i: (0,) * len(shape), pipeline_mode=pl.Buffered(1))


def split(whole, devices):
    chans, length = whole.shape
    piece = length // (devices * CHUNKS)
    return call(
        split_kernel,
        grid=(devices,),
        in_specs=[pl.BlockSpec((chans, piece * CHUNKS), lambda i: (0, i))],
        out_specs=[pl.BlockSpec((1, chans, piece), lambda i: (i, 0, 0))] * CHUNKS,
        out_shape=[jax.ShapeDtypeStruct((devices, chans, piece), whole.dtype)] * CHUNKS,
        name="split",
    )(whole)


def join(parts):
    devices, chans, piece = parts[0].shape
    return call(
        join_kernel,
        grid=(devices,),
        in_specs=[pl.BlockSpec((1, chans, piece), lambda i: (i, 0, 0))] * CHUNKS,
        out_specs=pl.BlockSpec((chans, piece * CHUNKS), lambda i: (0, i)),
        out_shape=jax.ShapeDtypeStruct((chans, devices * CHUNKS * piece), parts[0].dtype),
        name="join",
    )(*parts)


def mix(inputs, right, left, order, devices):
    chans, length = inputs.shape
    piece = length // (devices * CHUNKS)
    table = fixed((LB, LS, LS))
    strip = pl.BlockSpec((LANES, length), lambda i: (i, 0))
    results = call(
        mix_kernel,
        grid=(chans // LANES,),
        in_specs=[strip, table, table, fixed((LS, LS))],
        out_specs=[pl.BlockSpec((devices, LANES, piece), lambda i: (0, i, 0))] * CHUNKS
        + [strip, pl.BlockSpec((LB, LS, LANES), lambda i: (0, 0, i))],
        out_shape=[jax.ShapeDtypeStruct((devices, chans, piece), BF16)] * CHUNKS
        + [
            jax.ShapeDtypeStruct((chans, length), BF16),
            jax.ShapeDtypeStruct((LB, LS, chans), BF16),
        ],
        scratch_shapes=[pltpu.VMEM((length, LANES), F32)] * 2,
        name="mix",
    )(inputs, right, left, order)
    return results[:CHUNKS], results[CHUNKS], results[CHUNKS + 1]


def feature(hidden, above, right, right_back, left, left_back, order):
    total, piece = hidden.shape
    table = fixed((NB, BS, BS))
    strip = pl.BlockSpec((total, LANES), lambda i: (0, i))
    terms = pl.BlockSpec((NB, BS, BS), lambda i: (0, 0, 0))
    return call(
        feature_kernel,
        grid=(piece // LANES,),
        in_specs=[strip, strip, table, table, table, table, fixed((BS, BS))],
        out_specs=[strip, strip, terms, terms],
        out_shape=[jax.ShapeDtypeStruct((total, piece), BF16)] * 2
        + [jax.ShapeDtypeStruct((NB, BS, BS), F32)] * 2,
        scratch_shapes=[pltpu.VMEM((total, LANES), F32)] * 3
        + [pltpu.VMEM((NB, BS, LANES), BF16)],
        name="feature",
    )(hidden, above, right, right_back, left, left_back, order)


def back(inputs, time_mixed, first_mix, right, left_back, eye, grads):
    chans, length = inputs.shape
    devices, _, piece = grads[0].shape
    table = fixed((LB, LS, LS))
    strip = pl.BlockSpec((LANES, length), lambda i: (i, 0))
    terms = pl.BlockSpec((LB, LS, LS), lambda i: (0, 0, 0))
    return call(
        back_kernel,
        grid=(chans // LANES,),
        in_specs=[
            strip, strip, pl.BlockSpec((LB, LS, LANES), lambda i: (0, 0, i)),
            table, table, fixed((LS, LS)),
        ]
        + [pl.BlockSpec((devices, LANES, piece), lambda i: (0, i, 0))] * CHUNKS,
        out_specs=[strip, terms, terms],
        out_shape=[jax.ShapeDtypeStruct((chans, length), BF16)]
        + [jax.ShapeDtypeStruct((LB, LS, LS), F32)] * 2,
        scratch_shapes=[pltpu.VMEM((length, LANES), F32)] * 2,
        name="back",
    )(inputs, time_mixed, first_mix, right, left_back, eye, *grads)


def unfolded(table, axis, blocks):
    shape = table.shape
    fold = shape[axis] // blocks
    cut = table.reshape(shape[:axis] + (blocks, fold) + shape[axis + 1 :])
    return jnp.swapaxes(cut, axis, axis + 1).reshape(shape)


def folded(table, axis, fold):
    shape = table.shape
    cut = table.reshape(shape[:axis] + (fold, shape[axis] // fold) + shape[axis + 1 :])
    return jnp.swapaxes(cut, axis, axis + 1).reshape(shape)


def log2(size):
    return size.bit_length() - 1


def scatter_sum(terms, groups):
    blocks, size, width = terms[0].shape
    dp, mp = lax.axis_size("dp"), lax.axis_size("mp")

    def halve(parts, name, bit, outer, kind):
        count = lax.axis_size(name)
        mine = (lax.axis_index(name) >> bit) & 1
        parts = [part.reshape(outer, 2, -1, width) for part in parts]
        keep = sum(lax.dynamic_index_in_dim(part, mine, 1, keepdims=False) for part in parts)
        give = sum(lax.dynamic_index_in_dim(part, 1 - mine, 1, keepdims=False) for part in parts)
        got = lax.ppermute(give.astype(kind), name, [(i, i ^ (1 << bit)) for i in range(count)])
        return [keep + got.astype(F32)]

    for bit in range(log2(dp)):
        terms = halve(terms, "dp", bit, blocks * groups * (dp >> (bit + 1)), F32 if bit == 0 else BF16)
    for bit in range(log2(mp)):
        terms = halve(terms, "mp", bit, mp >> (bit + 1), BF16)
    return terms[0].reshape(blocks // mp, size // dp, width)


def gathered_tables(*tables):
    kinds = len(tables)
    share, size, width = tables[0].shape
    dp, mp = lax.axis_size("dp"), lax.axis_size("mp")
    cut = jnp.stack(tables).reshape(kinds, share, dp, size // dp, width)
    cut = lax.dynamic_index_in_dim(cut, lax.axis_index("dp"), 2, keepdims=False)
    full = lax.all_gather(cut, ("dp", "mp"), axis=0, tiled=False)
    full = full.reshape(dp, mp, kinds, share, size // dp, width).transpose(2, 1, 3, 0, 4, 5)
    return full.reshape(kinds, mp * share, size, width)


def on_device(inputs, cotangent, mixer_right, mixer_left, dense_right, dense_left):
    batch, chans, length = inputs.shape
    devices = lax.axis_size("mp")
    fold = LS // LB
    inputs = inputs.reshape(batch * chans, length)
    cotangent = cotangent.reshape(batch * chans, length)

    def exchange(part):
        shape = part.shape
        part = part.reshape(devices, chans, length // (devices * CHUNKS))
        return lax.all_to_all(part, "mp", 0, 0, tiled=True).reshape(shape)

    def rows(part):
        return part.reshape(devices * chans, -1)

    sent = split(cotangent, devices)
    sent, inputs, mixer_right, mixer_left = lax.optimization_barrier(
        (sent, inputs, mixer_right, mixer_left)
    )
    above = []
    for part in sent:
        if above:
            part, above[-1] = lax.optimization_barrier((part, above[-1]))
        above.append(exchange(part))

    eye = jnp.eye(LS, dtype=BF16)
    order = unfolded(eye, 0, LB)
    mix_right = unfolded(mixer_right, 2, LB).swapaxes(1, 2)
    mix_left_back = unfolded(unfolded(mixer_left, 1, LB), 2, LB)
    mix_left = mix_left_back.swapaxes(1, 2)
    right_back, left_back = gathered_tables(
        unfolded(dense_right, 2, NB), unfolded(unfolded(dense_left, 1, NB), 2, NB)
    )
    right, left = right_back.swapaxes(1, 2), left_back.swapaxes(1, 2)

    hidden, time_mixed, first_mix = mix(inputs, mix_right, mix_left, order, devices)
    tables = (right, right_back, left, left_back)
    hidden, above, tables = lax.optimization_barrier((hidden, above, tables))
    arrived = []
    for part in hidden:
        if arrived:
            part, arrived[-1] = lax.optimization_barrier((part, arrived[-1]))
        arrived.append(exchange(part))
    outs, grads, rights, lefts = [], [], [], []
    for part in range(CHUNKS):
        out, grad, term_right, term_left = feature(
            rows(arrived[part]), rows(above[part]), *tables, order.T
        )
        outs.append(out.reshape(devices, chans, -1))
        grad = grad.reshape(devices, chans, -1)
        if part:
            grad, grads[-1] = lax.optimization_barrier((grad, grads[-1]))
        grads.append(exchange(grad))
        rights.append(term_right)
        lefts.append(term_left)
    dense_rsum = scatter_sum(rights, 1)
    dense_lsum = scatter_sum(lefts, fold)
    grads, outs, dense_rsum, dense_lsum = lax.optimization_barrier(
        (grads, outs, dense_rsum, dense_lsum)
    )
    returned = [exchange(outs[0])]
    grad_inputs, term_right, term_left = back(
        inputs, time_mixed, first_mix, mix_right, mix_left_back, eye, grads
    )
    grad_inputs, term_right, term_left, outs, returned = lax.optimization_barrier(
        (grad_inputs, term_right, term_left, outs, returned)
    )
    for part in outs[1:]:
        part, returned[-1] = lax.optimization_barrier((part, returned[-1]))
        returned.append(exchange(part))
    mixer_rsum = scatter_sum([term_right], 1)
    mixer_lsum = scatter_sum([term_left], fold)
    block_out = join(returned)

    sequences = batch * lax.axis_size("dp")
    dense_scale = float(sequences * length) ** (-0.5)
    mixer_scale = float(sequences * chans * devices) ** (-0.5)
    return (
        block_out.reshape(batch, chans, length),
        grad_inputs.reshape(batch, chans, length),
        folded(mixer_rsum, 2, fold) * mixer_scale,
        folded(folded(mixer_lsum, 1, fold), 2, fold) * mixer_scale,
        folded(dense_rsum, 2, fold) * dense_scale,
        folded(folded(dense_lsum, 1, fold), 2, fold) * dense_scale,
    )


def solution(mesh):
    whole = P("dp", "mp", None)
    table = P("mp", None, None)
    return jax.shard_map(
        on_device,
        mesh=mesh,
        in_specs=(whole, whole, P(), P(), table, table),
        out_specs=(whole, whole) + (P("mp", "dp", None),) * 4,
        check_vma=False,
    )
```

```python
import functools

import jax
import jax.numpy as jnp
from jax import lax
from jax.experimental import pallas as pl
from jax.experimental.pallas import tpu as pltpu
from jax.sharding import PartitionSpec as P

NB = 64
BS = 128
LB = 64
LS = 128
LANES = 128
CHUNKS = 2
UNROLL = 4
VMEM = 60 * 1024 * 1024
F32 = jnp.float32
BF16 = jnp.bfloat16

NN = (((1,), (0,)), ((), ()))
NT = (((1,), (1,)), ((), ()))
TN = (((0,), (0,)), ((), ()))


def dot(left, right, dims=NN):
    return lax.dot_general(left, right, dims, preferred_element_type=F32)


def each(count, step, unroll=UNROLL):
    def group(index, carry):
        for inner in range(unroll):
            step(index * unroll + inner, inner)
        return carry

    lax.fori_loop(0, count // unroll, group, 0)


def block_of(index, size):
    return pl.ds(pl.multiple_of(index * size, size), size)


def gathered(ref, index, blocks, size):
    fold = size // blocks
    parts = [ref[pl.ds(f * blocks + index, blocks, stride=size), :] for f in range(fold)]
    return jnp.concatenate(parts, 0).astype(BF16)


def gathered_natural(ref, index, blocks, size):
    fold = size // blocks
    parts = [ref[pl.ds(index * fold + f, blocks, stride=size), :] for f in range(fold)]
    return jnp.concatenate(parts, 0).astype(BF16)


def mix_kernel(x_ref, right_ref, left_ref, order_ref, *refs):
    hidden_refs, (time_ref, first_ref, one, two) = refs[:CHUNKS], refs[CHUNKS:]

    def first(b, _):
        one[block_of(b, LS), :] = dot(right_ref[b], x_ref[:, block_of(b, LS)], NT)

    def second(e, _):
        rows = gathered(one, e, LB, LS)
        first_ref[e] = rows
        two[block_of(e, LS), :] = dot(left_ref[e], rows)

    devices, _, piece = hidden_refs[0].shape
    per_device = LB // devices
    per_chunk = piece // LS

    def third(e, inner):
        mixed = dot(gathered(two, e, LB, LS), order_ref[...], TN)
        time_ref[:, block_of(e, LS)] = mixed.astype(BF16)
        x = x_ref[:, block_of(e, LS)].astype(F32)
        hidden = x + x * jax.nn.sigmoid(x) * mixed.astype(BF16).astype(F32)
        place = pl.ds(inner % per_chunk * LS, LS)
        hidden_refs[inner // per_chunk][e // per_device, :, place] = hidden.astype(BF16)

    each(LB, first)
    each(LB, second)
    each(LB, third, per_device)


def feature_kernel(
    hidden_ref, above_ref, right_ref, right_back_ref, left_ref, left_back_ref, order_ref,
    out_ref, grad_ref, term_right_ref, term_left_ref, one, two, direct, panel,
):
    @pl.when(pl.program_id(0) == 0)
    def _():
        term_right_ref[...] = jnp.zeros_like(term_right_ref)
        term_left_ref[...] = jnp.zeros_like(term_left_ref)

    def first(b, _):
        one[block_of(b, BS), :] = dot(right_ref[b], hidden_ref[block_of(b, BS), :])

    def second(e, _):
        rows = gathered(one, e, NB, BS)
        panel[e] = rows
        two[block_of(e, BS), :] = dot(left_ref[e], rows)

    def third(e, _):
        rows = block_of(e, BS)
        gate = dot(order_ref[...], gathered(two, e, NB, BS))
        hidden = hidden_ref[rows, :].astype(F32)
        above = above_ref[rows, :].astype(F32)
        sigma = jax.nn.sigmoid(gate)
        through = 1.0 + gate * sigma
        slope = sigma * (1.0 + gate * (1.0 - sigma))
        out_ref[rows, :] = (hidden * through).astype(BF16)
        direct[rows, :] = above * through
        one[rows, :] = above * hidden * slope

    def fourth(e, _):
        rows = gathered_natural(one, e, NB, BS)
        two[block_of(e, BS), :] = dot(left_back_ref[e], rows)
        term_left_ref[e] += dot(panel[e], rows, NT)

    def fifth(b, _):
        rows = gathered(two, b, NB, BS)
        place = block_of(b, BS)
        grad_ref[place, :] = (direct[place, :] + dot(right_back_ref[b], rows)).astype(BF16)
        term_right_ref[b] += dot(hidden_ref[place, :], rows, NT)

    each(NB, first)
    each(NB, second)
    each(NB, third)
    each(NB, fourth)
    each(NB, fifth)


def back_kernel(x_ref, time_ref, first_ref, right_ref, left_back_ref, eye_ref, *refs):
    grad_refs = refs[:CHUNKS]
    out_ref, term_right_ref, term_left_ref, one, two = refs[CHUNKS:]
    devices, _, piece = grad_refs[0].shape
    per_device = LB // devices
    per_chunk = piece // LS

    @pl.when(pl.program_id(0) == 0)
    def _():
        term_right_ref[...] = jnp.zeros_like(term_right_ref)
        term_left_ref[...] = jnp.zeros_like(term_left_ref)

    def grad_of(e, inner):
        place = pl.ds(inner % per_chunk * LS, LS)
        return grad_refs[inner // per_chunk][e // per_device, :, place].astype(F32)

    def first(e, inner):
        x = x_ref[:, block_of(e, LS)].astype(F32)
        grad_time = (grad_of(e, inner) * (x * jax.nn.sigmoid(x))).astype(BF16)
        one[block_of(e, LS), :] = dot(eye_ref[...], grad_time, NT)

    def second(e, _):
        rows = gathered_natural(one, e, LB, LS)
        two[block_of(e, LS), :] = dot(left_back_ref[e], rows)
        term_left_ref[e] += dot(first_ref[e], rows, NT)

    def third(b, inner):
        place = block_of(b, LS)
        rows = gathered(two, b, LB, LS)
        x = x_ref[:, place]
        term = dot(rows, right_ref[b], TN)
        values = x.astype(F32)
        sigma = jax.nn.sigmoid(values)
        slope = sigma * (1.0 + values * (1.0 - sigma))
        grad = grad_of(b, inner)
        result = grad * (1.0 + slope * time_ref[:, place].astype(F32)) + term
        out_ref[:, place] = result.astype(BF16)
        term_right_ref[b] += lax.dot_general(
            x, rows, (((0,), (1,)), ((), ())), preferred_element_type=F32
        )

    each(LB, first, per_device)
    each(LB, second)
    each(LB, third, per_device)


def copy_kernel(from_ref, *refs):
    to_ref = refs[-1]
    to_ref[...] = from_ref[...].reshape(to_ref.shape)


def call(kernel, *args, **more):
    return pl.pallas_call(
        kernel, *args, compiler_params=pltpu.CompilerParams(vmem_limit_bytes=VMEM), **more
    )


def fixed(shape):
    return pl.BlockSpec(shape, lambda i: (0,) * len(shape), pipeline_mode=pl.Buffered(1))


def split(whole, devices, part):
    chans, length = whole.shape
    piece = length // (devices * CHUNKS)
    return call(
        copy_kernel,
        grid=(devices,),
        in_specs=[pl.BlockSpec((chans, piece), lambda i: (0, i * CHUNKS + part))],
        out_specs=pl.BlockSpec((1, chans, piece), lambda i: (i, 0, 0)),
        out_shape=jax.ShapeDtypeStruct((devices, chans, piece), whole.dtype),
        name="split",
    )(whole)


def join(piece_in, part, whole=None):
    devices, chans, piece = piece_in.shape
    shape = jax.ShapeDtypeStruct((chans, devices * CHUNKS * piece), piece_in.dtype)
    more, alias = ([], {}) if whole is None else ([whole], {1: 0})
    return call(
        copy_kernel,
        grid=(devices,),
        in_specs=[pl.BlockSpec((1, chans, piece), lambda i: (i, 0, 0))]
        + [pl.BlockSpec(memory_space=pl.ANY) for _ in more],
        out_specs=pl.BlockSpec((chans, piece), lambda i: (0, i * CHUNKS + part)),
        out_shape=shape,
        input_output_aliases=alias,
        name="join",
    )(piece_in, *more)


def mix(inputs, right, left, order, devices):
    chans, length = inputs.shape
    piece = length // (devices * CHUNKS)
    table = fixed((LB, LS, LS))
    strip = pl.BlockSpec((LANES, length), lambda i: (i, 0))
    results = call(
        mix_kernel,
        grid=(chans // LANES,),
        in_specs=[strip, table, table, fixed((LS, LS))],
        out_specs=[pl.BlockSpec((devices, LANES, piece), lambda i: (0, i, 0))] * CHUNKS
        + [strip, pl.BlockSpec((LB, LS, LANES), lambda i: (0, 0, i))],
        out_shape=[jax.ShapeDtypeStruct((devices, chans, piece), BF16)] * CHUNKS
        + [
            jax.ShapeDtypeStruct((chans, length), BF16),
            jax.ShapeDtypeStruct((LB, LS, chans), BF16),
        ],
        scratch_shapes=[pltpu.VMEM((length, LANES), F32)] * 2,
        name="mix",
    )(inputs, right, left, order)
    return results[:CHUNKS], results[CHUNKS], results[CHUNKS + 1]


def feature(hidden, above, right, right_back, left, left_back, order):
    total, piece = hidden.shape
    table = fixed((NB, BS, BS))
    strip = pl.BlockSpec((total, LANES), lambda i: (0, i))
    terms = pl.BlockSpec((NB, BS, BS), lambda i: (0, 0, 0))
    return call(
        feature_kernel,
        grid=(piece // LANES,),
        in_specs=[strip, strip, table, table, table, table, fixed((BS, BS))],
        out_specs=[strip, strip, terms, terms],
        out_shape=[jax.ShapeDtypeStruct((total, piece), BF16)] * 2
        + [jax.ShapeDtypeStruct((NB, BS, BS), F32)] * 2,
        scratch_shapes=[pltpu.VMEM((total, LANES), F32)] * 3
        + [pltpu.VMEM((NB, BS, LANES), BF16)],
        name="feature",
    )(hidden, above, right, right_back, left, left_back, order)


def back(inputs, time_mixed, first_mix, right, left_back, eye, grads):
    chans, length = inputs.shape
    devices, _, piece = grads[0].shape
    table = fixed((LB, LS, LS))
    strip = pl.BlockSpec((LANES, length), lambda i: (i, 0))
    terms = pl.BlockSpec((LB, LS, LS), lambda i: (0, 0, 0))
    return call(
        back_kernel,
        grid=(chans // LANES,),
        in_specs=[
            strip, strip, pl.BlockSpec((LB, LS, LANES), lambda i: (0, 0, i)),
            table, table, fixed((LS, LS)),
        ]
        + [pl.BlockSpec((devices, LANES, piece), lambda i: (0, i, 0))] * CHUNKS,
        out_specs=[strip, terms, terms],
        out_shape=[jax.ShapeDtypeStruct((chans, length), BF16)]
        + [jax.ShapeDtypeStruct((LB, LS, LS), F32)] * 2,
        scratch_shapes=[pltpu.VMEM((length, LANES), F32)] * 2,
        name="back",
    )(inputs, time_mixed, first_mix, right, left_back, eye, *grads)


def unfolded(table, axis, blocks):
    shape = table.shape
    fold = shape[axis] // blocks
    cut = table.reshape(shape[:axis] + (blocks, fold) + shape[axis + 1 :])
    return jnp.swapaxes(cut, axis, axis + 1).reshape(shape)


def folded(table, axis, fold):
    shape = table.shape
    cut = table.reshape(shape[:axis] + (fold, shape[axis] // fold) + shape[axis + 1 :])
    return jnp.swapaxes(cut, axis, axis + 1).reshape(shape)


def log2(size):
    return size.bit_length() - 1


def scatter_sum(terms, groups):
    blocks, size, width = terms[0].shape
    dp, mp = lax.axis_size("dp"), lax.axis_size("mp")

    def halve(parts, name, bit, outer, kind):
        count = lax.axis_size(name)
        mine = (lax.axis_index(name) >> bit) & 1
        parts = [part.reshape(outer, 2, -1, width) for part in parts]
        keep = sum(lax.dynamic_index_in_dim(part, mine, 1, keepdims=False) for part in parts)
        give = sum(lax.dynamic_index_in_dim(part, 1 - mine, 1, keepdims=False) for part in parts)
        got = lax.ppermute(give.astype(kind), name, [(i, i ^ (1 << bit)) for i in range(count)])
        return [keep + got.astype(F32)]

    for bit in range(log2(dp)):
        terms = halve(terms, "dp", bit, blocks * groups * (dp >> (bit + 1)), F32 if bit == 0 else BF16)
    for bit in range(log2(mp)):
        terms = halve(terms, "mp", bit, mp >> (bit + 1), BF16)
    return terms[0].reshape(blocks // mp, size // dp, width)


def gathered_tables(*tables):
    kinds = len(tables)
    share, size, width = tables[0].shape
    dp, mp = lax.axis_size("dp"), lax.axis_size("mp")
    rows = size // dp
    cut = jnp.stack(tables).reshape(kinds * share, dp, rows, width)
    cut = lax.dynamic_index_in_dim(cut, lax.axis_index("dp"), 1, keepdims=False)

    def double(full, name, bit, axis):
        count = lax.axis_size(name)
        got = lax.ppermute(full, name, [(i, i ^ (1 << bit)) for i in range(count)])
        upper = (lax.axis_index(name) >> bit) & 1 == 1
        return jnp.where(upper, jnp.stack([got, full], axis), jnp.stack([full, got], axis))

    full = cut[None]
    for bit in reversed(range(log2(mp))):
        full = double(full, "mp", bit, 1).reshape(-1, kinds * share, rows, width)
    full = full.reshape(mp * kinds * share, 1, rows, width)
    for bit in reversed(range(log2(dp))):
        full = double(full, "dp", bit, 2).reshape(mp * kinds * share, -1, rows, width)
    full = full.reshape(mp, kinds, share, size, width)
    return [full[:, kind].reshape(mp * share, size, width) for kind in range(kinds)]


def on_device(inputs, cotangent, mixer_right, mixer_left, dense_right, dense_left):
    batch, chans, length = inputs.shape
    devices = lax.axis_size("mp")
    fold = LS // LB
    inputs = inputs.reshape(batch * chans, length)
    cotangent = cotangent.reshape(batch * chans, length)

    def exchange(part):
        shape = part.shape
        part = part.reshape(devices, chans, length // (devices * CHUNKS))
        return lax.all_to_all(part, "mp", 0, 0, tiled=True).reshape(shape)

    def rows(part):
        return part.reshape(devices * chans, -1)

    right_back, left_back = gathered_tables(
        unfolded(dense_right, 2, NB), unfolded(unfolded(dense_left, 1, NB), 2, NB)
    )
    above = []
    for part in range(CHUNKS):
        sent = split(cotangent, devices, part)
        if part:
            sent, above[-1] = lax.optimization_barrier((sent, above[-1]))
        else:
            sent, cotangent, inputs, mixer_right, mixer_left = lax.optimization_barrier(
                (sent, cotangent, inputs, mixer_right, mixer_left)
            )
        above.append(exchange(sent))

    eye = jnp.eye(LS, dtype=BF16)
    order = unfolded(eye, 0, LB)
    mix_right = unfolded(mixer_right, 2, LB).swapaxes(1, 2)
    mix_left_back = unfolded(unfolded(mixer_left, 1, LB), 2, LB)
    mix_left = mix_left_back.swapaxes(1, 2)
    right, left = right_back.swapaxes(1, 2), left_back.swapaxes(1, 2)

    hidden, time_mixed, first_mix = mix(inputs, mix_right, mix_left, order, devices)
    tables = (right, right_back, left, left_back)
    hidden, above, tables = lax.optimization_barrier((hidden, above, tables))
    arrived = []
    for part in hidden:
        if arrived:
            part, arrived[-1] = lax.optimization_barrier((part, arrived[-1]))
        arrived.append(exchange(part))
    outs, grads, rights, lefts = [], [], [], []
    for part in range(CHUNKS):
        out, grad, term_right, term_left = feature(
            rows(arrived[part]), rows(above[part]), *tables, order.T
        )
        outs.append(out.reshape(devices, chans, -1))
        grad = grad.reshape(devices, chans, -1)
        if part:
            grad, grads[-1] = lax.optimization_barrier((grad, grads[-1]))
        grads.append(exchange(grad))
        rights.append(term_right)
        lefts.append(term_left)
    dense_rsum = scatter_sum(rights, 1)
    dense_lsum = scatter_sum(lefts, fold)
    grads, outs, dense_rsum, dense_lsum = lax.optimization_barrier(
        (grads, outs, dense_rsum, dense_lsum)
    )
    returned = [exchange(outs[0])]
    grad_inputs, term_right, term_left = back(
        inputs, time_mixed, first_mix, mix_right, mix_left_back, eye, grads
    )
    grad_inputs, term_right, term_left, outs, returned = lax.optimization_barrier(
        (grad_inputs, term_right, term_left, outs, returned)
    )
    for part in outs[1:]:
        part, returned[-1] = lax.optimization_barrier((part, returned[-1]))
        returned.append(exchange(part))
    mixer_rsum = scatter_sum([term_right], 1)
    mixer_lsum = scatter_sum([term_left], fold)
    block_out = None
    for part in range(CHUNKS):
        block_out = join(returned[part], part, block_out)

    sequences = batch * lax.axis_size("dp")
    dense_scale = float(sequences * length) ** (-0.5)
    mixer_scale = float(sequences * chans * devices) ** (-0.5)
    return (
        block_out.reshape(batch, chans, length),
        grad_inputs.reshape(batch, chans, length),
        folded(mixer_rsum, 2, fold) * mixer_scale,
        folded(folded(mixer_lsum, 1, fold), 2, fold) * mixer_scale,
        folded(dense_rsum, 2, fold) * dense_scale,
        folded(folded(dense_lsum, 1, fold), 2, fold) * dense_scale,
    )


def solution(mesh):
    whole = P("dp", "mp", None)
    table = P("mp", None, None)
    return jax.shard_map(
        on_device,
        mesh=mesh,
        in_specs=(whole, whole, P(), P(), table, table),
        out_specs=(whole, whole) + (P("mp", "dp", None),) * 4,
        check_vma=False,
    )
```

```python
import functools

import jax
import jax.numpy as jnp
from jax import lax
from jax.experimental import pallas as pl
from jax.experimental.pallas import tpu as pltpu
from jax.sharding import PartitionSpec as P

NB = 64
BS = 128
LB = 64
LS = 128
LANES = 128
CHUNKS = 2
NEAR = 4
UNROLL = 4
VMEM = 60 * 1024 * 1024
F32 = jnp.float32
BF16 = jnp.bfloat16

NN = (((1,), (0,)), ((), ()))
NT = (((1,), (1,)), ((), ()))
TN = (((0,), (0,)), ((), ()))


def dot(left, right, dims=NN):
    return lax.dot_general(left, right, dims, preferred_element_type=F32)


def each(count, step, unroll=UNROLL):
    def group(index, carry):
        for inner in range(unroll):
            step(index * unroll + inner, inner)
        return carry

    lax.fori_loop(0, count // unroll, group, 0)


def block_of(index, size):
    return pl.ds(pl.multiple_of(index * size, size), size)


def gathered(ref, index, blocks, size):
    fold = size // blocks
    parts = [ref[pl.ds(f * blocks + index, blocks, stride=size), :] for f in range(fold)]
    return jnp.concatenate(parts, 0).astype(BF16)


def gathered_natural(ref, index, blocks, size):
    fold = size // blocks
    parts = [ref[pl.ds(index * fold + f, blocks, stride=size), :] for f in range(fold)]
    return jnp.concatenate(parts, 0).astype(BF16)


def mix_kernel(x_ref, right_ref, left_ref, order_ref, *refs):
    hidden_refs, (time_ref, first_ref, one, two) = refs[:CHUNKS], refs[CHUNKS:]

    def first(b, _):
        one[block_of(b, LS), :] = dot(right_ref[b], x_ref[:, block_of(b, LS)], NT)

    def second(e, _):
        rows = gathered(one, e, LB, LS)
        first_ref[e] = rows
        two[block_of(e, LS), :] = dot(left_ref[e], rows)

    devices, _, piece = hidden_refs[0].shape
    per_device = LB // devices
    per_chunk = piece // LS

    def third(e, inner):
        mixed = dot(gathered(two, e, LB, LS), order_ref[...], TN)
        time_ref[:, block_of(e, LS)] = mixed.astype(BF16)
        x = x_ref[:, block_of(e, LS)].astype(F32)
        hidden = x + x * jax.nn.sigmoid(x) * mixed.astype(BF16).astype(F32)
        place = pl.ds(inner % per_chunk * LS, LS)
        hidden_refs[inner // per_chunk][e // per_device, :, place] = hidden.astype(BF16)

    each(LB, first)
    each(LB, second)
    each(LB, third, per_device)


def feature_kernel(
    hidden_ref, above_ref, right_ref, right_back_ref, left_ref, left_back_ref, order_ref,
    out_ref, grad_ref, term_right_ref, term_left_ref, one, two, direct, panel,
):
    @pl.when(pl.program_id(0) == 0)
    def _():
        term_right_ref[...] = jnp.zeros_like(term_right_ref)
        term_left_ref[...] = jnp.zeros_like(term_left_ref)

    def first(b, _):
        one[block_of(b, BS), :] = dot(right_ref[b], hidden_ref[block_of(b, BS), :])

    def second(e, _):
        rows = gathered(one, e, NB, BS)
        panel[e] = rows
        two[block_of(e, BS), :] = dot(left_ref[e], rows)

    def third(e, _):
        rows = block_of(e, BS)
        gate = dot(order_ref[...], gathered(two, e, NB, BS))
        hidden = hidden_ref[rows, :].astype(F32)
        above = above_ref[rows, :].astype(F32)
        sigma = jax.nn.sigmoid(gate)
        through = 1.0 + gate * sigma
        slope = sigma * (1.0 + gate * (1.0 - sigma))
        out_ref[rows, :] = (hidden * through).astype(BF16)
        direct[rows, :] = above * through
        one[rows, :] = above * hidden * slope

    def fourth(e, _):
        rows = gathered_natural(one, e, NB, BS)
        two[block_of(e, BS), :] = dot(left_back_ref[e], rows)
        term_left_ref[e] += dot(panel[e], rows, NT)

    def fifth(b, _):
        rows = gathered(two, b, NB, BS)
        place = block_of(b, BS)
        grad_ref[place, :] = (direct[place, :] + dot(right_back_ref[b], rows)).astype(BF16)
        term_right_ref[b] += dot(hidden_ref[place, :], rows, NT)

    each(NB, first)
    each(NB, second)
    each(NB, third)
    each(NB, fourth)
    each(NB, fifth)


def back_kernel(x_ref, time_ref, first_ref, right_ref, left_back_ref, eye_ref, *refs):
    grad_refs = refs[:CHUNKS]
    out_ref, term_right_ref, term_left_ref, one, two = refs[CHUNKS:]
    devices, _, piece = grad_refs[0].shape
    per_device = LB // devices
    per_chunk = piece // LS

    @pl.when(pl.program_id(0) == 0)
    def _():
        term_right_ref[...] = jnp.zeros_like(term_right_ref)
        term_left_ref[...] = jnp.zeros_like(term_left_ref)

    def grad_of(e, inner):
        place = pl.ds(inner % per_chunk * LS, LS)
        return grad_refs[inner // per_chunk][e // per_device, :, place].astype(F32)

    def first(e, inner):
        x = x_ref[:, block_of(e, LS)].astype(F32)
        grad_time = (grad_of(e, inner) * (x * jax.nn.sigmoid(x))).astype(BF16)
        one[block_of(e, LS), :] = dot(eye_ref[...], grad_time, NT)

    def second(e, _):
        rows = gathered_natural(one, e, LB, LS)
        two[block_of(e, LS), :] = dot(left_back_ref[e], rows)
        term_left_ref[e] += dot(first_ref[e], rows, NT)

    def third(b, inner):
        place = block_of(b, LS)
        rows = gathered(two, b, LB, LS)
        x = x_ref[:, place]
        term = dot(rows, right_ref[b], TN)
        values = x.astype(F32)
        sigma = jax.nn.sigmoid(values)
        slope = sigma * (1.0 + values * (1.0 - sigma))
        grad = grad_of(b, inner)
        result = grad * (1.0 + slope * time_ref[:, place].astype(F32)) + term
        out_ref[:, place] = result.astype(BF16)
        term_right_ref[b] += lax.dot_general(
            x, rows, (((0,), (1,)), ((), ())), preferred_element_type=F32
        )

    each(LB, first, per_device)
    each(LB, second)
    each(LB, third, per_device)


def move(pairs, held, arrive_sems, leave_sems):
    arrive, leave = [], []
    for index, (source, _) in enumerate(pairs):
        arrive.append(pltpu.make_async_copy(source, held.at[index], arrive_sems.at[index]))
        arrive[-1].start()
    for index, (_, target) in enumerate(pairs):
        arrive[index].wait()
        leave.append(pltpu.make_async_copy(held.at[index], target, leave_sems.at[index]))
        leave[-1].start()
    for copy in leave:
        copy.wait()


def places(whole_ref, part, devices, piece):
    return [whole_ref.at[:, pl.ds((d * CHUNKS + part) * piece, piece)] for d in range(devices)]


def split_kernel(part, whole_ref, part_ref, *scratch):
    devices, _, piece = part_ref.shape
    sources = places(whole_ref, part, devices, piece)
    move([(sources[d], part_ref.at[d]) for d in range(devices)], *scratch)


def join_kernel(part, part_ref, *refs):
    whole_ref, scratch = refs[-4], refs[-3:]
    devices, _, piece = part_ref.shape
    targets = places(whole_ref, part, devices, piece)
    move([(part_ref.at[d], targets[d]) for d in range(devices)], *scratch)


def call(kernel, *args, **more):
    return pl.pallas_call(
        kernel, *args, compiler_params=pltpu.CompilerParams(vmem_limit_bytes=VMEM), **more
    )


def fixed(shape):
    return pl.BlockSpec(shape, lambda i: (0,) * len(shape), pipeline_mode=pl.Buffered(1))


def moving(devices, chans, piece):
    return [pltpu.VMEM((devices, chans, piece), BF16)] + [pltpu.SemaphoreType.DMA((devices,))] * 2


def split(whole, devices, part):
    chans, length = whole.shape
    piece = length // (devices * CHUNKS)
    return call(
        functools.partial(split_kernel, part),
        in_specs=[pl.BlockSpec(memory_space=pl.ANY)],
        out_specs=pl.BlockSpec(memory_space=pl.ANY),
        out_shape=jax.ShapeDtypeStruct((devices, chans, piece), whole.dtype),
        scratch_shapes=moving(devices, chans, piece),
        name="split",
    )(whole)


def join(piece_in, part, whole=None):
    devices, chans, piece = piece_in.shape
    args = [piece_in] if whole is None else [piece_in, whole]
    return call(
        functools.partial(join_kernel, part),
        in_specs=[pl.BlockSpec(memory_space=pl.ANY)] * len(args),
        out_specs=pl.BlockSpec(memory_space=pl.ANY),
        out_shape=jax.ShapeDtypeStruct((chans, devices * CHUNKS * piece), piece_in.dtype),
        scratch_shapes=moving(devices, chans, piece),
        input_output_aliases={} if whole is None else {1: 0},
        name="join",
    )(*args)


def mix(inputs, right, left, order, devices):
    chans, length = inputs.shape
    piece = length // (devices * CHUNKS)
    table = fixed((LB, LS, LS))
    strip = pl.BlockSpec((LANES, length), lambda i: (i, 0))
    results = call(
        mix_kernel,
        grid=(chans // LANES,),
        in_specs=[strip, table, table, fixed((LS, LS))],
        out_specs=[pl.BlockSpec((devices, LANES, piece), lambda i: (0, i, 0))] * CHUNKS
        + [strip, pl.BlockSpec((LB, LS, LANES), lambda i: (0, 0, i))],
        out_shape=[jax.ShapeDtypeStruct((devices, chans, piece), BF16)] * CHUNKS
        + [
            jax.ShapeDtypeStruct((chans, length), BF16),
            jax.ShapeDtypeStruct((LB, LS, chans), BF16),
        ],
        scratch_shapes=[pltpu.VMEM((length, LANES), F32)] * 2,
        name="mix",
    )(inputs, right, left, order)
    return results[:CHUNKS], results[CHUNKS], results[CHUNKS + 1]


def feature(hidden, above, right, right_back, left, left_back, order):
    total, piece = hidden.shape
    table = fixed((NB, BS, BS))
    strip = pl.BlockSpec((total, LANES), lambda i: (0, i))
    terms = pl.BlockSpec((NB, BS, BS), lambda i: (0, 0, 0))
    return call(
        feature_kernel,
        grid=(piece // LANES,),
        in_specs=[strip, strip, table, table, table, table, fixed((BS, BS))],
        out_specs=[strip, strip, terms, terms],
        out_shape=[jax.ShapeDtypeStruct((total, piece), BF16)] * 2
        + [jax.ShapeDtypeStruct((NB, BS, BS), F32)] * 2,
        scratch_shapes=[pltpu.VMEM((total, LANES), F32)] * 3
        + [pltpu.VMEM((NB, BS, LANES), BF16)],
        name="feature",
    )(hidden, above, right, right_back, left, left_back, order)


def back(inputs, time_mixed, first_mix, right, left_back, eye, grads):
    chans, length = inputs.shape
    devices, _, piece = grads[0].shape
    table = fixed((LB, LS, LS))
    strip = pl.BlockSpec((LANES, length), lambda i: (i, 0))
    terms = pl.BlockSpec((LB, LS, LS), lambda i: (0, 0, 0))
    return call(
        back_kernel,
        grid=(chans // LANES,),
        in_specs=[
            strip, strip, pl.BlockSpec((LB, LS, LANES), lambda i: (0, 0, i)),
            table, table, fixed((LS, LS)),
        ]
        + [pl.BlockSpec((devices, LANES, piece), lambda i: (0, i, 0))] * CHUNKS,
        out_specs=[strip, terms, terms],
        out_shape=[jax.ShapeDtypeStruct((chans, length), BF16)]
        + [jax.ShapeDtypeStruct((LB, LS, LS), F32)] * 2,
        scratch_shapes=[pltpu.VMEM((length, LANES), F32)] * 2,
        name="back",
    )(inputs, time_mixed, first_mix, right, left_back, eye, *grads)


def unfolded(table, axis, blocks):
    shape = table.shape
    fold = shape[axis] // blocks
    cut = table.reshape(shape[:axis] + (blocks, fold) + shape[axis + 1 :])
    return jnp.swapaxes(cut, axis, axis + 1).reshape(shape)


def folded(table, axis, fold):
    shape = table.shape
    cut = table.reshape(shape[:axis] + (fold, shape[axis] // fold) + shape[axis + 1 :])
    return jnp.swapaxes(cut, axis, axis + 1).reshape(shape)


def log2(size):
    return size.bit_length() - 1


def scatter_sum(terms, groups):
    blocks, size, width = terms[0].shape
    dp, mp = lax.axis_size("dp"), lax.axis_size("mp")

    def halve(parts, name, bit, outer, kind):
        count = lax.axis_size(name)
        mine = (lax.axis_index(name) >> bit) & 1
        parts = [part.reshape(outer, 2, -1, width) for part in parts]
        keep = sum(lax.dynamic_index_in_dim(part, mine, 1, keepdims=False) for part in parts)
        give = sum(lax.dynamic_index_in_dim(part, 1 - mine, 1, keepdims=False) for part in parts)
        got = lax.ppermute(give.astype(kind), name, [(i, i ^ (1 << bit)) for i in range(count)])
        return [keep + got.astype(F32)]

    for bit in range(log2(dp)):
        terms = halve(terms, "dp", bit, blocks * groups * (dp >> (bit + 1)), F32 if bit == 0 else BF16)
    for bit in range(log2(NEAR)):
        terms = halve(terms, "mp", bit, mp >> (bit + 1), BF16)
    far = mp // NEAR
    place = lax.axis_index("mp") // NEAR
    parts = terms[0].reshape(far, blocks // mp * (size // dp), width)
    total = lax.dynamic_index_in_dim(parts, place, 0, keepdims=False)
    got = []
    for step in range(1, far):
        give = lax.dynamic_index_in_dim(parts, (place + step) % far, 0, keepdims=False)
        got.append(lax.ppermute(give.astype(BF16), "mp", far_pairs(mp, step)))
    for part in got:
        total = total + part.astype(F32)
    return total.reshape(blocks // mp, size // dp, width)


def far_pairs(mp, step):
    return [(i, (i // NEAR + step) % (mp // NEAR) * NEAR + i % NEAR) for i in range(mp)]


def far_tables(*tables):
    share, size, width = tables[0].shape
    dp, mp = lax.axis_size("dp"), lax.axis_size("mp")
    cut = jnp.stack(tables).reshape(len(tables), share, dp, size // dp, width)
    cut = lax.dynamic_index_in_dim(cut, lax.axis_index("dp"), 2, keepdims=False)
    return [cut] + [lax.ppermute(cut, "mp", far_pairs(mp, k)) for k in range(1, mp // NEAR)]


def all_tables(parts):
    dp, mp = lax.axis_size("dp"), lax.axis_size("mp")
    far, place = mp // NEAR, lax.axis_index("mp") // NEAR
    kinds, share, rows, width = parts[0].shape
    parts = jnp.stack(parts)
    full = [
        lax.dynamic_index_in_dim(parts, (place - z) % far, 0, keepdims=False) for z in range(far)
    ]
    planes = [[z * NEAR + n for n in range(NEAR)] for z in range(far)]
    full = lax.all_gather(jnp.stack(full), "mp", axis=0, tiled=False, axis_index_groups=planes)
    full = lax.all_gather(full, "dp", axis=0, tiled=False)
    full = full.transpose(3, 2, 1, 4, 0, 5, 6)
    return full.reshape(kinds, mp * share, dp * rows, width)


def on_device(inputs, cotangent, mixer_right, mixer_left, dense_right, dense_left):
    batch, chans, length = inputs.shape
    devices = lax.axis_size("mp")
    fold = LS // LB
    inputs = inputs.reshape(batch * chans, length)
    cotangent = cotangent.reshape(batch * chans, length)

    def exchange(part):
        shape = part.shape
        part = part.reshape(devices, chans, length // (devices * CHUNKS))
        return lax.all_to_all(part, "mp", 0, 0, tiled=True).reshape(shape)

    def rows(part):
        return part.reshape(devices * chans, -1)

    tables = far_tables(dense_right, dense_left)
    sent = split(cotangent, devices, 0)
    sent, tables, cotangent, inputs, mixer_right, mixer_left = lax.optimization_barrier(
        (sent, tables, cotangent, inputs, mixer_right, mixer_left)
    )
    above = [exchange(sent)]

    eye = jnp.eye(LS, dtype=BF16)
    order = unfolded(eye, 0, LB)
    mix_right = unfolded(mixer_right, 2, LB).swapaxes(1, 2)
    mix_left_back = unfolded(unfolded(mixer_left, 1, LB), 2, LB)
    mix_left = mix_left_back.swapaxes(1, 2)
    hidden, time_mixed, first_mix = mix(inputs, mix_right, mix_left, order, devices)
    for part in range(1, CHUNKS):
        sent = split(cotangent, devices, part)
        sent, above[-1], hidden, tables = lax.optimization_barrier(
            (sent, above[-1], hidden, tables)
        )
        above.append(exchange(sent))
    dense_right, dense_left = all_tables(tables)
    right_back = unfolded(dense_right, 2, NB)
    left_back = unfolded(unfolded(dense_left, 1, NB), 2, NB)
    tables = (right_back.swapaxes(1, 2), right_back, left_back.swapaxes(1, 2), left_back)
    hidden, above, tables = lax.optimization_barrier((hidden, above, tables))
    arrived = []
    for part in hidden:
        if arrived:
            part, arrived[-1] = lax.optimization_barrier((part, arrived[-1]))
        arrived.append(exchange(part))
    outs, grads, rights, lefts = [], [], [], []
    for part in range(CHUNKS):
        out, grad, term_right, term_left = feature(
            rows(arrived[part]), rows(above[part]), *tables, order.T
        )
        outs.append(out.reshape(devices, chans, -1))
        grad = grad.reshape(devices, chans, -1)
        if part:
            grad, grads[-1] = lax.optimization_barrier((grad, grads[-1]))
        grads.append(exchange(grad))
        rights.append(term_right)
        lefts.append(term_left)
    dense_rsum = scatter_sum(rights, 1)
    dense_lsum = scatter_sum(lefts, fold)
    grads, outs, dense_rsum, dense_lsum = lax.optimization_barrier(
        (grads, outs, dense_rsum, dense_lsum)
    )
    returned = [exchange(outs[0])]
    grad_inputs, term_right, term_left = back(
        inputs, time_mixed, first_mix, mix_right, mix_left_back, eye, grads
    )
    grad_inputs, term_right, term_left, outs, returned = lax.optimization_barrier(
        (grad_inputs, term_right, term_left, outs, returned)
    )
    for part in outs[1:]:
        part, returned[-1] = lax.optimization_barrier((part, returned[-1]))
        returned.append(exchange(part))
    mixer_rsum = scatter_sum([term_right], 1)
    mixer_lsum = scatter_sum([term_left], fold)
    block_out = None
    for part in range(CHUNKS):
        block_out = join(returned[part], part, block_out)

    sequences = batch * lax.axis_size("dp")
    dense_scale = float(sequences * length) ** (-0.5)
    mixer_scale = float(sequences * chans * devices) ** (-0.5)
    return (
        block_out.reshape(batch, chans, length),
        grad_inputs.reshape(batch, chans, length),
        folded(mixer_rsum, 2, fold) * mixer_scale,
        folded(folded(mixer_lsum, 1, fold), 2, fold) * mixer_scale,
        folded(dense_rsum, 2, fold) * dense_scale,
        folded(folded(dense_lsum, 1, fold), 2, fold) * dense_scale,
    )


def solution(mesh):
    whole = P("dp", "mp", None)
    table = P("mp", None, None)
    return jax.shard_map(
        on_device,
        mesh=mesh,
        in_specs=(whole, whole, P(), P(), table, table),
        out_specs=(whole, whole) + (P("mp", "dp", None),) * 4,
        check_vma=False,
    )
```

```python
import functools

import jax
import jax.numpy as jnp
from jax import lax
from jax.experimental import pallas as pl
from jax.experimental.pallas import tpu as pltpu
from jax.sharding import PartitionSpec as P

NB = 64
BS = 128
LB = 64
LS = 128
LANES = 128
CHUNKS = 2
NEAR = 4
UNROLL = 4
VMEM = 60 * 1024 * 1024
F32 = jnp.float32
BF16 = jnp.bfloat16

NN = (((1,), (0,)), ((), ()))
NT = (((1,), (1,)), ((), ()))
TN = (((0,), (0,)), ((), ()))


def dot(left, right, dims=NN):
    return lax.dot_general(left, right, dims, preferred_element_type=F32)


def each(count, step, unroll=UNROLL):
    def group(index, carry):
        for inner in range(unroll):
            step(index * unroll + inner, inner)
        return carry

    lax.fori_loop(0, count // unroll, group, 0)


def block_of(index, size):
    return pl.ds(pl.multiple_of(index * size, size), size)


def gathered(ref, index, blocks, size):
    fold = size // blocks
    parts = [ref[pl.ds(f * blocks + index, blocks, stride=size), :] for f in range(fold)]
    return jnp.concatenate(parts, 0).astype(BF16)


def gathered_natural(ref, index, blocks, size):
    fold = size // blocks
    parts = [ref[pl.ds(index * fold + f, blocks, stride=size), :] for f in range(fold)]
    return jnp.concatenate(parts, 0).astype(BF16)


def mix_kernel(x_ref, right_ref, left_ref, order_ref, *refs):
    hidden_refs, (time_ref, first_ref, one, two) = refs[:CHUNKS], refs[CHUNKS:]

    def first(b, _):
        one[block_of(b, LS), :] = dot(right_ref[b], x_ref[:, block_of(b, LS)], NT)

    def second(e, _):
        rows = gathered(one, e, LB, LS)
        first_ref[e] = rows
        two[block_of(e, LS), :] = dot(left_ref[e], rows)

    devices, _, piece = hidden_refs[0].shape
    per_device = LB // devices
    per_chunk = piece // LS

    def third(e, inner):
        mixed = dot(gathered(two, e, LB, LS), order_ref[...], TN)
        time_ref[:, block_of(e, LS)] = mixed.astype(BF16)
        x = x_ref[:, block_of(e, LS)].astype(F32)
        hidden = x + x * jax.nn.sigmoid(x) * mixed.astype(BF16).astype(F32)
        place = pl.ds(inner % per_chunk * LS, LS)
        hidden_refs[inner // per_chunk][e // per_device, :, place] = hidden.astype(BF16)

    each(LB, first)
    each(LB, second)
    each(LB, third, per_device)


def feature_kernel(
    hidden_ref, above_ref, right_ref, right_back_ref, left_ref, left_back_ref, order_ref,
    out_ref, grad_ref, term_right_ref, term_left_ref, one, two, direct, panel,
):
    @pl.when(pl.program_id(0) == 0)
    def _():
        term_right_ref[...] = jnp.zeros_like(term_right_ref)
        term_left_ref[...] = jnp.zeros_like(term_left_ref)

    def first(b, _):
        one[block_of(b, BS), :] = dot(right_ref[b], hidden_ref[block_of(b, BS), :])

    def second(e, _):
        rows = gathered(one, e, NB, BS)
        panel[e] = rows
        two[block_of(e, BS), :] = dot(left_ref[e], rows)

    def third(e, _):
        rows = block_of(e, BS)
        gate = dot(order_ref[...], gathered(two, e, NB, BS))
        hidden = hidden_ref[rows, :].astype(F32)
        above = above_ref[rows, :].astype(F32)
        sigma = jax.nn.sigmoid(gate)
        through = 1.0 + gate * sigma
        slope = sigma * (1.0 + gate * (1.0 - sigma))
        out_ref[rows, :] = (hidden * through).astype(BF16)
        direct[rows, :] = above * through
        one[rows, :] = above * hidden * slope

    def fourth(e, _):
        rows = gathered_natural(one, e, NB, BS)
        two[block_of(e, BS), :] = dot(left_back_ref[e], rows)
        term_left_ref[e] += dot(panel[e], rows, NT)

    def fifth(b, _):
        rows = gathered(two, b, NB, BS)
        place = block_of(b, BS)
        grad_ref[place, :] = (direct[place, :] + dot(right_back_ref[b], rows)).astype(BF16)
        term_right_ref[b] += dot(hidden_ref[place, :], rows, NT)

    each(NB, first)
    each(NB, second)
    each(NB, third)
    each(NB, fourth)
    each(NB, fifth)


def back_kernel(x_ref, time_ref, first_ref, right_ref, left_back_ref, eye_ref, *refs):
    grad_refs = refs[:CHUNKS]
    out_ref, term_right_ref, term_left_ref, one, two = refs[CHUNKS:]
    devices, _, piece = grad_refs[0].shape
    per_device = LB // devices
    per_chunk = piece // LS

    @pl.when(pl.program_id(0) == 0)
    def _():
        term_right_ref[...] = jnp.zeros_like(term_right_ref)
        term_left_ref[...] = jnp.zeros_like(term_left_ref)

    def grad_of(e, inner):
        place = pl.ds(inner % per_chunk * LS, LS)
        return grad_refs[inner // per_chunk][e // per_device, :, place].astype(F32)

    def first(e, inner):
        x = x_ref[:, block_of(e, LS)].astype(F32)
        grad_time = (grad_of(e, inner) * (x * jax.nn.sigmoid(x))).astype(BF16)
        one[block_of(e, LS), :] = dot(eye_ref[...], grad_time, NT)

    def second(e, _):
        rows = gathered_natural(one, e, LB, LS)
        two[block_of(e, LS), :] = dot(left_back_ref[e], rows)
        term_left_ref[e] += dot(first_ref[e], rows, NT)

    def third(b, inner):
        place = block_of(b, LS)
        rows = gathered(two, b, LB, LS)
        x = x_ref[:, place]
        term = dot(rows, right_ref[b], TN)
        values = x.astype(F32)
        sigma = jax.nn.sigmoid(values)
        slope = sigma * (1.0 + values * (1.0 - sigma))
        grad = grad_of(b, inner)
        result = grad * (1.0 + slope * time_ref[:, place].astype(F32)) + term
        out_ref[:, place] = result.astype(BF16)
        term_right_ref[b] += lax.dot_general(
            x, rows, (((0,), (1,)), ((), ())), preferred_element_type=F32
        )

    each(LB, first, per_device)
    each(LB, second)
    each(LB, third, per_device)


def move(pairs, held, arrive_sems, leave_sems):
    arrive, leave = [], []
    for index, (source, _) in enumerate(pairs):
        arrive.append(pltpu.make_async_copy(source, held.at[index], arrive_sems.at[index]))
        arrive[-1].start()
    for index, (_, target) in enumerate(pairs):
        arrive[index].wait()
        leave.append(pltpu.make_async_copy(held.at[index], target, leave_sems.at[index]))
        leave[-1].start()
    for copy in leave:
        copy.wait()


def places(whole_ref, part, devices, piece):
    return [whole_ref.at[:, pl.ds((d * CHUNKS + part) * piece, piece)] for d in range(devices)]


def split_kernel(part, whole_ref, part_ref, *scratch):
    devices, _, piece = part_ref.shape
    sources = places(whole_ref, part, devices, piece)
    move([(sources[d], part_ref.at[d]) for d in range(devices)], *scratch)


def join_kernel(part, part_ref, *refs):
    whole_ref, scratch = refs[-4], refs[-3:]
    devices, _, piece = part_ref.shape
    targets = places(whole_ref, part, devices, piece)
    move([(part_ref.at[d], targets[d]) for d in range(devices)], *scratch)


def call(kernel, *args, **more):
    return pl.pallas_call(
        kernel, *args, compiler_params=pltpu.CompilerParams(vmem_limit_bytes=VMEM), **more
    )


def fixed(shape):
    return pl.BlockSpec(shape, lambda i: (0,) * len(shape), pipeline_mode=pl.Buffered(1))


def moving(devices, chans, piece):
    return [pltpu.VMEM((devices, chans, piece), BF16)] + [pltpu.SemaphoreType.DMA((devices,))] * 2


def split(whole, devices, part):
    chans, length = whole.shape
    piece = length // (devices * CHUNKS)
    return call(
        functools.partial(split_kernel, part),
        in_specs=[pl.BlockSpec(memory_space=pl.ANY)],
        out_specs=pl.BlockSpec(memory_space=pl.ANY),
        out_shape=jax.ShapeDtypeStruct((devices, chans, piece), whole.dtype),
        scratch_shapes=moving(devices, chans, piece),
        name="split",
    )(whole)


def join(piece_in, part, whole=None):
    devices, chans, piece = piece_in.shape
    args = [piece_in] if whole is None else [piece_in, whole]
    return call(
        functools.partial(join_kernel, part),
        in_specs=[pl.BlockSpec(memory_space=pl.ANY)] * len(args),
        out_specs=pl.BlockSpec(memory_space=pl.ANY),
        out_shape=jax.ShapeDtypeStruct((chans, devices * CHUNKS * piece), piece_in.dtype),
        scratch_shapes=moving(devices, chans, piece),
        input_output_aliases={} if whole is None else {1: 0},
        name="join",
    )(*args)


def mix(inputs, right, left, order, devices):
    chans, length = inputs.shape
    piece = length // (devices * CHUNKS)
    table = fixed((LB, LS, LS))
    strip = pl.BlockSpec((LANES, length), lambda i: (i, 0))
    results = call(
        mix_kernel,
        grid=(chans // LANES,),
        in_specs=[strip, table, table, fixed((LS, LS))],
        out_specs=[pl.BlockSpec((devices, LANES, piece), lambda i: (0, i, 0))] * CHUNKS
        + [strip, pl.BlockSpec((LB, LS, LANES), lambda i: (0, 0, i))],
        out_shape=[jax.ShapeDtypeStruct((devices, chans, piece), BF16)] * CHUNKS
        + [
            jax.ShapeDtypeStruct((chans, length), BF16),
            jax.ShapeDtypeStruct((LB, LS, chans), BF16),
        ],
        scratch_shapes=[pltpu.VMEM((length, LANES), F32)] * 2,
        name="mix",
    )(inputs, right, left, order)
    return results[:CHUNKS], results[CHUNKS], results[CHUNKS + 1]


def feature(hidden, above, right, right_back, left, left_back, order):
    total, piece = hidden.shape
    table = fixed((NB, BS, BS))
    strip = pl.BlockSpec((total, LANES), lambda i: (0, i))
    terms = pl.BlockSpec((NB, BS, BS), lambda i: (0, 0, 0))
    return call(
        feature_kernel,
        grid=(piece // LANES,),
        in_specs=[strip, strip, table, table, table, table, fixed((BS, BS))],
        out_specs=[strip, strip, terms, terms],
        out_shape=[jax.ShapeDtypeStruct((total, piece), BF16)] * 2
        + [jax.ShapeDtypeStruct((NB, BS, BS), F32)] * 2,
        scratch_shapes=[pltpu.VMEM((total, LANES), F32)] * 3
        + [pltpu.VMEM((NB, BS, LANES), BF16)],
        name="feature",
    )(hidden, above, right, right_back, left, left_back, order)


def back(inputs, time_mixed, first_mix, right, left_back, eye, grads):
    chans, length = inputs.shape
    devices, _, piece = grads[0].shape
    table = fixed((LB, LS, LS))
    strip = pl.BlockSpec((LANES, length), lambda i: (i, 0))
    terms = pl.BlockSpec((LB, LS, LS), lambda i: (0, 0, 0))
    return call(
        back_kernel,
        grid=(chans // LANES,),
        in_specs=[
            strip, strip, pl.BlockSpec((LB, LS, LANES), lambda i: (0, 0, i)),
            table, table, fixed((LS, LS)),
        ]
        + [pl.BlockSpec((devices, LANES, piece), lambda i: (0, i, 0))] * CHUNKS,
        out_specs=[strip, terms, terms],
        out_shape=[jax.ShapeDtypeStruct((chans, length), BF16)]
        + [jax.ShapeDtypeStruct((LB, LS, LS), F32)] * 2,
        scratch_shapes=[pltpu.VMEM((length, LANES), F32)] * 2,
        name="back",
    )(inputs, time_mixed, first_mix, right, left_back, eye, *grads)


def unfolded(table, axis, blocks):
    shape = table.shape
    fold = shape[axis] // blocks
    cut = table.reshape(shape[:axis] + (blocks, fold) + shape[axis + 1 :])
    return jnp.swapaxes(cut, axis, axis + 1).reshape(shape)


def folded(table, axis, fold):
    shape = table.shape
    cut = table.reshape(shape[:axis] + (fold, shape[axis] // fold) + shape[axis + 1 :])
    return jnp.swapaxes(cut, axis, axis + 1).reshape(shape)


def log2(size):
    return size.bit_length() - 1


def scatter_sum(terms, groups):
    blocks, size, width = terms[0].shape
    dp, mp = lax.axis_size("dp"), lax.axis_size("mp")

    def halve(parts, name, bit, outer, kind):
        count = lax.axis_size(name)
        mine = (lax.axis_index(name) >> bit) & 1
        parts = [part.reshape(outer, 2, -1, width) for part in parts]
        keep = sum(lax.dynamic_index_in_dim(part, mine, 1, keepdims=False) for part in parts)
        give = sum(lax.dynamic_index_in_dim(part, 1 - mine, 1, keepdims=False) for part in parts)
        got = lax.ppermute(give.astype(kind), name, [(i, i ^ (1 << bit)) for i in range(count)])
        return [keep + got.astype(F32)]

    for bit in range(log2(dp)):
        terms = halve(terms, "dp", bit, blocks * groups * (dp >> (bit + 1)), F32 if bit == 0 else BF16)
    for bit in range(log2(mp)):
        terms = halve(terms, "mp", bit, mp >> (bit + 1), BF16)
    return terms[0].reshape(blocks // mp, size // dp, width)


def far_pairs(mp, step):
    return [(i, (i // NEAR + step) % (mp // NEAR) * NEAR + i % NEAR) for i in range(mp)]


def far_tables(*tables):
    share, size, width = tables[0].shape
    dp, mp = lax.axis_size("dp"), lax.axis_size("mp")
    cut = jnp.stack(tables).reshape(len(tables), share, dp, size // dp, width)
    cut = lax.dynamic_index_in_dim(cut, lax.axis_index("dp"), 2, keepdims=False)
    return [cut] + [lax.ppermute(cut, "mp", far_pairs(mp, k)) for k in range(1, mp // NEAR)]


def near_tables(parts):
    mp = lax.axis_size("mp")
    far, place = mp // NEAR, lax.axis_index("mp") // NEAR
    parts = jnp.stack(parts)
    full = [
        lax.dynamic_index_in_dim(parts, (place - z) % far, 0, keepdims=False) for z in range(far)
    ]
    planes = [[z * NEAR + n for n in range(NEAR)] for z in range(far)]
    return lax.all_gather(jnp.stack(full), "mp", axis=0, tiled=False, axis_index_groups=planes)


def all_tables(full):
    full = lax.all_gather(full, "dp", axis=0, tiled=False)
    dp, near, far, kinds, share, rows, width = full.shape
    full = full.transpose(3, 2, 1, 4, 0, 5, 6)
    return full.reshape(kinds, near * far * share, dp * rows, width)


def on_device(inputs, cotangent, mixer_right, mixer_left, dense_right, dense_left):
    batch, chans, length = inputs.shape
    devices = lax.axis_size("mp")
    fold = LS // LB
    inputs = inputs.reshape(batch * chans, length)
    cotangent = cotangent.reshape(batch * chans, length)

    def exchange(part):
        shape = part.shape
        part = part.reshape(devices, chans, length // (devices * CHUNKS))
        return lax.all_to_all(part, "mp", 0, 0, tiled=True).reshape(shape)

    def rows(part):
        return part.reshape(devices * chans, -1)

    tables = far_tables(dense_right, dense_left)
    sent = split(cotangent, devices, 0)
    sent, tables, cotangent, inputs, mixer_right, mixer_left = lax.optimization_barrier(
        (sent, tables, cotangent, inputs, mixer_right, mixer_left)
    )
    above = [exchange(sent)]

    eye = jnp.eye(LS, dtype=BF16)
    order = unfolded(eye, 0, LB)
    mix_right = unfolded(mixer_right, 2, LB).swapaxes(1, 2)
    mix_left_back = unfolded(unfolded(mixer_left, 1, LB), 2, LB)
    mix_left = mix_left_back.swapaxes(1, 2)
    hidden, time_mixed, first_mix = mix(inputs, mix_right, mix_left, order, devices)
    for part in range(1, CHUNKS):
        sent = split(cotangent, devices, part)
        sent, above[-1], hidden, tables = lax.optimization_barrier(
            (sent, above[-1], hidden, tables)
        )
        above.append(exchange(sent))
    hidden, above, tables = lax.optimization_barrier((hidden, above, near_tables(tables)))
    dense_right, dense_left = all_tables(tables)
    right_back = unfolded(dense_right, 2, NB)
    left_back = unfolded(unfolded(dense_left, 1, NB), 2, NB)
    tables = (right_back.swapaxes(1, 2), right_back, left_back.swapaxes(1, 2), left_back)
    arrived = []
    for part in hidden:
        if arrived:
            part, arrived[-1], tables = lax.optimization_barrier((part, arrived[-1], tables))
        arrived.append(exchange(part))
    outs, grads, rights, lefts = [], [], [], []
    for part in range(CHUNKS):
        out, grad, term_right, term_left = feature(
            rows(arrived[part]), rows(above[part]), *tables, order.T
        )
        outs.append(out.reshape(devices, chans, -1))
        grad = grad.reshape(devices, chans, -1)
        if part:
            grad, grads[-1] = lax.optimization_barrier((grad, grads[-1]))
        grads.append(exchange(grad))
        rights.append(term_right)
        lefts.append(term_left)
    dense_rsum = scatter_sum(rights, 1)
    dense_lsum = scatter_sum(lefts, fold)
    grads, outs, dense_rsum, dense_lsum = lax.optimization_barrier(
        (grads, outs, dense_rsum, dense_lsum)
    )
    returned = [exchange(outs[0])]
    grad_inputs, term_right, term_left = back(
        inputs, time_mixed, first_mix, mix_right, mix_left_back, eye, grads
    )
    grad_inputs, term_right, term_left, outs, returned = lax.optimization_barrier(
        (grad_inputs, term_right, term_left, outs, returned)
    )
    for part in outs[1:]:
        part, returned[-1] = lax.optimization_barrier((part, returned[-1]))
        returned.append(exchange(part))
    mixer_rsum = scatter_sum([term_right], 1)
    mixer_lsum = scatter_sum([term_left], fold)
    block_out = None
    for part in range(CHUNKS):
        block_out = join(returned[part], part, block_out)

    sequences = batch * lax.axis_size("dp")
    dense_scale = float(sequences * length) ** (-0.5)
    mixer_scale = float(sequences * chans * devices) ** (-0.5)
    return (
        block_out.reshape(batch, chans, length),
        grad_inputs.reshape(batch, chans, length),
        folded(mixer_rsum, 2, fold) * mixer_scale,
        folded(folded(mixer_lsum, 1, fold), 2, fold) * mixer_scale,
        folded(dense_rsum, 2, fold) * dense_scale,
        folded(folded(dense_lsum, 1, fold), 2, fold) * dense_scale,
    )


def solution(mesh):
    whole = P("dp", "mp", None)
    table = P("mp", None, None)
    return jax.shard_map(
        on_device,
        mesh=mesh,
        in_specs=(whole, whole, P(), P(), table, table),
        out_specs=(whole, whole) + (P("mp", "dp", None),) * 4,
        check_vma=False,
    )
```

```python
import functools

import jax
import jax.numpy as jnp
from jax import lax
from jax.experimental import pallas as pl
from jax.experimental.pallas import tpu as pltpu
from jax.sharding import PartitionSpec as P

NB = 64
BS = 128
LB = 64
LS = 128
LANES = 128
CHUNKS = 2
NEAR = 4
UNROLL = 4
VMEM = 60 * 1024 * 1024
F32 = jnp.float32
BF16 = jnp.bfloat16

NN = (((1,), (0,)), ((), ()))
NT = (((1,), (1,)), ((), ()))
TN = (((0,), (0,)), ((), ()))


def dot(left, right, dims=NN):
    return lax.dot_general(left, right, dims, preferred_element_type=F32)


def each(count, step, unroll=UNROLL):
    def group(index, carry):
        for inner in range(unroll):
            step(index * unroll + inner, inner)
        return carry

    lax.fori_loop(0, count // unroll, group, 0)


def block_of(index, size):
    return pl.ds(pl.multiple_of(index * size, size), size)


def gathered(ref, index, blocks, size):
    fold = size // blocks
    parts = [ref[pl.ds(f * blocks + index, blocks, stride=size), :] for f in range(fold)]
    return jnp.concatenate(parts, 0).astype(BF16)


def gathered_natural(ref, index, blocks, size):
    fold = size // blocks
    parts = [ref[pl.ds(index * fold + f, blocks, stride=size), :] for f in range(fold)]
    return jnp.concatenate(parts, 0).astype(BF16)


def mix_kernel(x_ref, right_ref, left_ref, order_ref, *refs):
    hidden_refs, (time_ref, first_ref, one, two) = refs[:CHUNKS], refs[CHUNKS:]

    def first(b, _):
        one[block_of(b, LS), :] = dot(right_ref[b], x_ref[:, block_of(b, LS)], NT)

    def second(e, _):
        rows = gathered(one, e, LB, LS)
        first_ref[e] = rows
        two[block_of(e, LS), :] = dot(left_ref[e], rows)

    devices, _, piece = hidden_refs[0].shape
    per_device = LB // devices
    per_chunk = piece // LS

    def third(e, inner):
        mixed = dot(gathered(two, e, LB, LS), order_ref[...], TN)
        time_ref[:, block_of(e, LS)] = mixed.astype(BF16)
        x = x_ref[:, block_of(e, LS)].astype(F32)
        hidden = x + x * jax.nn.sigmoid(x) * mixed.astype(BF16).astype(F32)
        place = pl.ds(inner % per_chunk * LS, LS)
        hidden_refs[inner // per_chunk][e // per_device, :, place] = hidden.astype(BF16)

    each(LB, first)
    each(LB, second)
    each(LB, third, per_device)


def feature_kernel(
    hidden_ref, above_ref, right_ref, right_back_ref, left_ref, left_back_ref, order_ref,
    out_ref, grad_ref, term_right_ref, term_left_ref, one, two, direct, panel,
):
    @pl.when(pl.program_id(0) == 0)
    def _():
        term_right_ref[...] = jnp.zeros_like(term_right_ref)
        term_left_ref[...] = jnp.zeros_like(term_left_ref)

    def first(b, _):
        one[block_of(b, BS), :] = dot(right_ref[b], hidden_ref[block_of(b, BS), :])

    def second(e, _):
        rows = gathered(one, e, NB, BS)
        panel[e] = rows
        two[block_of(e, BS), :] = dot(left_ref[e], rows)

    def third(e, _):
        rows = block_of(e, BS)
        gate = dot(order_ref[...], gathered(two, e, NB, BS))
        hidden = hidden_ref[rows, :].astype(F32)
        above = above_ref[rows, :].astype(F32)
        sigma = jax.nn.sigmoid(gate)
        through = 1.0 + gate * sigma
        slope = sigma * (1.0 + gate * (1.0 - sigma))
        out_ref[rows, :] = (hidden * through).astype(BF16)
        direct[rows, :] = above * through
        one[rows, :] = above * hidden * slope

    def fourth(e, _):
        rows = gathered_natural(one, e, NB, BS)
        two[block_of(e, BS), :] = dot(left_back_ref[e], rows)
        term_left_ref[e] += dot(panel[e], rows, NT)

    def fifth(b, _):
        rows = gathered(two, b, NB, BS)
        place = block_of(b, BS)
        grad_ref[place, :] = (direct[place, :] + dot(right_back_ref[b], rows)).astype(BF16)
        term_right_ref[b] += dot(hidden_ref[place, :], rows, NT)

    each(NB, first)
    each(NB, second)
    each(NB, third)
    each(NB, fourth)
    each(NB, fifth)


def back_kernel(x_ref, time_ref, first_ref, right_ref, left_back_ref, eye_ref, *refs):
    grad_refs = refs[:CHUNKS]
    out_ref, term_right_ref, term_left_ref, one, two = refs[CHUNKS:]
    devices, _, piece = grad_refs[0].shape
    per_device = LB // devices
    per_chunk = piece // LS

    @pl.when(pl.program_id(0) == 0)
    def _():
        term_right_ref[...] = jnp.zeros_like(term_right_ref)
        term_left_ref[...] = jnp.zeros_like(term_left_ref)

    def grad_of(e, inner):
        place = pl.ds(inner % per_chunk * LS, LS)
        return grad_refs[inner // per_chunk][e // per_device, :, place].astype(F32)

    def first(e, inner):
        x = x_ref[:, block_of(e, LS)].astype(F32)
        grad_time = (grad_of(e, inner) * (x * jax.nn.sigmoid(x))).astype(BF16)
        one[block_of(e, LS), :] = dot(eye_ref[...], grad_time, NT)

    def second(e, _):
        rows = gathered_natural(one, e, LB, LS)
        two[block_of(e, LS), :] = dot(left_back_ref[e], rows)
        term_left_ref[e] += dot(first_ref[e], rows, NT)

    def third(b, inner):
        place = block_of(b, LS)
        rows = gathered(two, b, LB, LS)
        x = x_ref[:, place]
        term = dot(rows, right_ref[b], TN)
        values = x.astype(F32)
        sigma = jax.nn.sigmoid(values)
        slope = sigma * (1.0 + values * (1.0 - sigma))
        grad = grad_of(b, inner)
        result = grad * (1.0 + slope * time_ref[:, place].astype(F32)) + term
        out_ref[:, place] = result.astype(BF16)
        term_right_ref[b] += lax.dot_general(
            x, rows, (((0,), (1,)), ((), ())), preferred_element_type=F32
        )

    each(LB, first, per_device)
    each(LB, second)
    each(LB, third, per_device)


def move(pairs, held, arrive_sems, leave_sems):
    arrive, leave = [], []
    for index, (source, _) in enumerate(pairs):
        arrive.append(pltpu.make_async_copy(source, held.at[index], arrive_sems.at[index]))
        arrive[-1].start()
    for index, (_, target) in enumerate(pairs):
        arrive[index].wait()
        leave.append(pltpu.make_async_copy(held.at[index], target, leave_sems.at[index]))
        leave[-1].start()
    for copy in leave:
        copy.wait()


def places(whole_ref, part, devices, piece):
    return [whole_ref.at[:, pl.ds((d * CHUNKS + part) * piece, piece)] for d in range(devices)]


def split_kernel(part, whole_ref, part_ref, *scratch):
    devices, _, piece = part_ref.shape
    sources = places(whole_ref, part, devices, piece)
    move([(sources[d], part_ref.at[d]) for d in range(devices)], *scratch)


def join_kernel(part, part_ref, *refs):
    whole_ref, scratch = refs[-4], refs[-3:]
    devices, _, piece = part_ref.shape
    targets = places(whole_ref, part, devices, piece)
    move([(part_ref.at[d], targets[d]) for d in range(devices)], *scratch)


def call(kernel, *args, **more):
    return pl.pallas_call(
        kernel, *args, compiler_params=pltpu.CompilerParams(vmem_limit_bytes=VMEM), **more
    )


def fixed(shape):
    return pl.BlockSpec(shape, lambda i: (0,) * len(shape), pipeline_mode=pl.Buffered(1))


def moving(devices, chans, piece):
    return [pltpu.VMEM((devices, chans, piece), BF16)] + [pltpu.SemaphoreType.DMA((devices,))] * 2


def split(whole, devices, part):
    chans, length = whole.shape
    piece = length // (devices * CHUNKS)
    return call(
        functools.partial(split_kernel, part),
        in_specs=[pl.BlockSpec(memory_space=pl.ANY)],
        out_specs=pl.BlockSpec(memory_space=pl.ANY),
        out_shape=jax.ShapeDtypeStruct((devices, chans, piece), whole.dtype),
        scratch_shapes=moving(devices, chans, piece),
        name="split",
    )(whole)


def join(piece_in, part, whole=None):
    devices, chans, piece = piece_in.shape
    args = [piece_in] if whole is None else [piece_in, whole]
    return call(
        functools.partial(join_kernel, part),
        in_specs=[pl.BlockSpec(memory_space=pl.ANY)] * len(args),
        out_specs=pl.BlockSpec(memory_space=pl.ANY),
        out_shape=jax.ShapeDtypeStruct((chans, devices * CHUNKS * piece), piece_in.dtype),
        scratch_shapes=moving(devices, chans, piece),
        input_output_aliases={} if whole is None else {1: 0},
        name="join",
    )(*args)


def mix(inputs, right, left, order, devices):
    chans, length = inputs.shape
    piece = length // (devices * CHUNKS)
    table = fixed((LB, LS, LS))
    strip = pl.BlockSpec((LANES, length), lambda i: (i, 0))
    results = call(
        mix_kernel,
        grid=(chans // LANES,),
        in_specs=[strip, table, table, fixed((LS, LS))],
        out_specs=[pl.BlockSpec((devices, LANES, piece), lambda i: (0, i, 0))] * CHUNKS
        + [strip, pl.BlockSpec((LB, LS, LANES), lambda i: (0, 0, i))],
        out_shape=[jax.ShapeDtypeStruct((devices, chans, piece), BF16)] * CHUNKS
        + [
            jax.ShapeDtypeStruct((chans, length), BF16),
            jax.ShapeDtypeStruct((LB, LS, chans), BF16),
        ],
        scratch_shapes=[pltpu.VMEM((length, LANES), F32)] * 2,
        name="mix",
    )(inputs, right, left, order)
    return results[:CHUNKS], results[CHUNKS], results[CHUNKS + 1]


def feature(hidden, above, right, right_back, left, left_back, order):
    total, piece = hidden.shape
    table = fixed((NB, BS, BS))
    strip = pl.BlockSpec((total, LANES), lambda i: (0, i))
    terms = pl.BlockSpec((NB, BS, BS), lambda i: (0, 0, 0))
    return call(
        feature_kernel,
        grid=(piece // LANES,),
        in_specs=[strip, strip, table, table, table, table, fixed((BS, BS))],
        out_specs=[strip, strip, terms, terms],
        out_shape=[jax.ShapeDtypeStruct((total, piece), BF16)] * 2
        + [jax.ShapeDtypeStruct((NB, BS, BS), F32)] * 2,
        scratch_shapes=[pltpu.VMEM((total, LANES), F32)] * 3
        + [pltpu.VMEM((NB, BS, LANES), BF16)],
        name="feature",
    )(hidden, above, right, right_back, left, left_back, order)


def back(inputs, time_mixed, first_mix, right, left_back, eye, grads):
    chans, length = inputs.shape
    devices, _, piece = grads[0].shape
    table = fixed((LB, LS, LS))
    strip = pl.BlockSpec((LANES, length), lambda i: (i, 0))
    terms = pl.BlockSpec((LB, LS, LS), lambda i: (0, 0, 0))
    return call(
        back_kernel,
        grid=(chans // LANES,),
        in_specs=[
            strip, strip, pl.BlockSpec((LB, LS, LANES), lambda i: (0, 0, i)),
            table, table, fixed((LS, LS)),
        ]
        + [pl.BlockSpec((devices, LANES, piece), lambda i: (0, i, 0))] * CHUNKS,
        out_specs=[strip, terms, terms],
        out_shape=[jax.ShapeDtypeStruct((chans, length), BF16)]
        + [jax.ShapeDtypeStruct((LB, LS, LS), F32)] * 2,
        scratch_shapes=[pltpu.VMEM((length, LANES), F32)] * 2,
        name="back",
    )(inputs, time_mixed, first_mix, right, left_back, eye, *grads)


def unfolded(table, axis, blocks):
    shape = table.shape
    fold = shape[axis] // blocks
    cut = table.reshape(shape[:axis] + (blocks, fold) + shape[axis + 1 :])
    return jnp.swapaxes(cut, axis, axis + 1).reshape(shape)


def folded(table, axis, fold):
    shape = table.shape
    cut = table.reshape(shape[:axis] + (fold, shape[axis] // fold) + shape[axis + 1 :])
    return jnp.swapaxes(cut, axis, axis + 1).reshape(shape)


def log2(size):
    return size.bit_length() - 1


def scatter_sum(terms, groups):
    blocks, size, width = terms[0].shape
    dp, mp = lax.axis_size("dp"), lax.axis_size("mp")

    def halve(parts, name, bit, outer, kind):
        count = lax.axis_size(name)
        mine = (lax.axis_index(name) >> bit) & 1
        parts = [part.reshape(outer, 2, -1, width) for part in parts]
        keep = sum(lax.dynamic_index_in_dim(part, mine, 1, keepdims=False) for part in parts)
        give = sum(lax.dynamic_index_in_dim(part, 1 - mine, 1, keepdims=False) for part in parts)
        got = lax.ppermute(give.astype(kind), name, [(i, i ^ (1 << bit)) for i in range(count)])
        return [keep + got.astype(F32)]

    for bit in range(log2(dp)):
        terms = halve(terms, "dp", bit, blocks * groups * (dp >> (bit + 1)), F32 if bit == 0 else BF16)
    for bit in range(log2(mp)):
        terms = halve(terms, "mp", bit, mp >> (bit + 1), BF16)
    return terms[0].reshape(blocks // mp, size // dp, width)


def swapped(full, bit):
    mp = lax.axis_size("mp")
    return lax.ppermute(full, "mp", [(i, i ^ (1 << bit)) for i in range(mp)])


def doubled(full, got, bit):
    upper = (lax.axis_index("mp") >> bit) & 1 == 1
    both = jnp.where(upper, jnp.stack([got, full], 1), jnp.stack([full, got], 1))
    return both.reshape((-1,) + full.shape[1:])


def far_tables(*tables):
    share, size, width = tables[0].shape
    dp, mp = lax.axis_size("dp"), lax.axis_size("mp")
    cut = jnp.stack(tables).reshape(len(tables), share, dp, size // dp, width)
    cut = lax.dynamic_index_in_dim(cut, lax.axis_index("dp"), 2, keepdims=False)[None]
    return cut, swapped(cut, log2(mp) - 1)


def column_tables(cut, got):
    top = log2(lax.axis_size("mp")) - 1
    full = doubled(cut, got, top)
    for bit in reversed(range(log2(NEAR), top)):
        full = doubled(full, swapped(full, bit), bit)
    return full


def near_tables(full):
    far = lax.axis_size("mp") // NEAR
    planes = [[z * NEAR + n for n in range(NEAR)] for z in range(far)]
    return lax.all_gather(full, "mp", axis=0, tiled=False, axis_index_groups=planes)


def all_tables(full):
    full = lax.all_gather(full, "dp", axis=0, tiled=False)
    dp, near, far, kinds, share, rows, width = full.shape
    full = full.transpose(3, 2, 1, 4, 0, 5, 6)
    return full.reshape(kinds, near * far * share, dp * rows, width)


def on_device(inputs, cotangent, mixer_right, mixer_left, dense_right, dense_left):
    batch, chans, length = inputs.shape
    devices = lax.axis_size("mp")
    fold = LS // LB
    inputs = inputs.reshape(batch * chans, length)
    cotangent = cotangent.reshape(batch * chans, length)

    def exchange(part):
        shape = part.shape
        part = part.reshape(devices, chans, length // (devices * CHUNKS))
        return lax.all_to_all(part, "mp", 0, 0, tiled=True).reshape(shape)

    def rows(part):
        return part.reshape(devices * chans, -1)

    tables = far_tables(dense_right, dense_left)
    sent = split(cotangent, devices, 0)
    sent, tables, cotangent, inputs, mixer_right, mixer_left = lax.optimization_barrier(
        (sent, tables, cotangent, inputs, mixer_right, mixer_left)
    )
    above = [exchange(sent)]
    tables = column_tables(*tables)

    eye = jnp.eye(LS, dtype=BF16)
    order = unfolded(eye, 0, LB)
    mix_right = unfolded(mixer_right, 2, LB).swapaxes(1, 2)
    mix_left_back = unfolded(unfolded(mixer_left, 1, LB), 2, LB)
    mix_left = mix_left_back.swapaxes(1, 2)
    hidden, time_mixed, first_mix = mix(inputs, mix_right, mix_left, order, devices)
    for part in range(1, CHUNKS):
        sent = split(cotangent, devices, part)
        sent, above[-1], hidden, tables = lax.optimization_barrier(
            (sent, above[-1], hidden, tables)
        )
        above.append(exchange(sent))
    hidden, above, tables = lax.optimization_barrier((hidden, above, near_tables(tables)))
    dense_right, dense_left = all_tables(tables)
    right_back = unfolded(dense_right, 2, NB)
    left_back = unfolded(unfolded(dense_left, 1, NB), 2, NB)
    tables = (right_back.swapaxes(1, 2), right_back, left_back.swapaxes(1, 2), left_back)
    arrived = []
    for part in hidden:
        if arrived:
            part, arrived[-1], tables = lax.optimization_barrier((part, arrived[-1], tables))
        arrived.append(exchange(part))
    outs, grads, rights, lefts = [], [], [], []
    for part in range(CHUNKS):
        out, grad, term_right, term_left = feature(
            rows(arrived[part]), rows(above[part]), *tables, order.T
        )
        outs.append(out.reshape(devices, chans, -1))
        grad = grad.reshape(devices, chans, -1)
        if part:
            grad, grads[-1] = lax.optimization_barrier((grad, grads[-1]))
        grads.append(exchange(grad))
        rights.append(term_right)
        lefts.append(term_left)
    dense_rsum = scatter_sum(rights, 1)
    dense_lsum = scatter_sum(lefts, fold)
    grads, outs, dense_rsum, dense_lsum = lax.optimization_barrier(
        (grads, outs, dense_rsum, dense_lsum)
    )
    returned = [exchange(outs[0])]
    grad_inputs, term_right, term_left = back(
        inputs, time_mixed, first_mix, mix_right, mix_left_back, eye, grads
    )
    grad_inputs, term_right, term_left, outs, returned = lax.optimization_barrier(
        (grad_inputs, term_right, term_left, outs, returned)
    )
    for part in outs[1:]:
        part, returned[-1] = lax.optimization_barrier((part, returned[-1]))
        returned.append(exchange(part))
    mixer_rsum = scatter_sum([term_right], 1)
    mixer_lsum = scatter_sum([term_left], fold)
    block_out = None
    for part in range(CHUNKS):
        block_out = join(returned[part], part, block_out)

    sequences = batch * lax.axis_size("dp")
    dense_scale = float(sequences * length) ** (-0.5)
    mixer_scale = float(sequences * chans * devices) ** (-0.5)
    return (
        block_out.reshape(batch, chans, length),
        grad_inputs.reshape(batch, chans, length),
        folded(mixer_rsum, 2, fold) * mixer_scale,
        folded(folded(mixer_lsum, 1, fold), 2, fold) * mixer_scale,
        folded(dense_rsum, 2, fold) * dense_scale,
        folded(folded(dense_lsum, 1, fold), 2, fold) * dense_scale,
    )


def solution(mesh):
    whole = P("dp", "mp", None)
    table = P("mp", None, None)
    return jax.shard_map(
        on_device,
        mesh=mesh,
        in_specs=(whole, whole, P(), P(), table, table),
        out_specs=(whole, whole) + (P("mp", "dp", None),) * 4,
        check_vma=False,
    )
```

```python
import functools

import jax
import jax.numpy as jnp
from jax import lax
from jax.experimental import pallas as pl
from jax.experimental.pallas import tpu as pltpu
from jax.sharding import PartitionSpec as P

NB = 64
BS = 128
LB = 64
LS = 128
LANES = 128
CHUNKS = 2
NEAR = 4
UNROLL = 4
VMEM = 60 * 1024 * 1024
F32 = jnp.float32
BF16 = jnp.bfloat16

NN = (((1,), (0,)), ((), ()))
NT = (((1,), (1,)), ((), ()))
TN = (((0,), (0,)), ((), ()))


def dot(left, right, dims=NN):
    return lax.dot_general(left, right, dims, preferred_element_type=F32)


def each(count, step, unroll=UNROLL):
    def group(index, carry):
        for inner in range(unroll):
            step(index * unroll + inner, inner)
        return carry

    lax.fori_loop(0, count // unroll, group, 0)


def block_of(index, size):
    return pl.ds(pl.multiple_of(index * size, size), size)


def gathered(ref, index, blocks, size):
    fold = size // blocks
    parts = [ref[pl.ds(f * blocks + index, blocks, stride=size), :] for f in range(fold)]
    return jnp.concatenate(parts, 0).astype(BF16)


def gathered_natural(ref, index, blocks, size):
    fold = size // blocks
    parts = [ref[pl.ds(index * fold + f, blocks, stride=size), :] for f in range(fold)]
    return jnp.concatenate(parts, 0).astype(BF16)


def mix_kernel(x_ref, right_ref, left_ref, order_ref, *refs):
    hidden_refs, (time_ref, first_ref, one, two) = refs[:CHUNKS], refs[CHUNKS:]

    def first(b, _):
        one[block_of(b, LS), :] = dot(right_ref[b], x_ref[:, block_of(b, LS)], NT)

    def second(e, _):
        rows = gathered(one, e, LB, LS)
        first_ref[e] = rows
        two[block_of(e, LS), :] = dot(left_ref[e], rows)

    devices, _, piece = hidden_refs[0].shape
    per_device = LB // devices
    per_chunk = piece // LS

    def third(e, inner):
        mixed = dot(gathered(two, e, LB, LS), order_ref[...], TN)
        time_ref[:, block_of(e, LS)] = mixed.astype(BF16)
        x = x_ref[:, block_of(e, LS)].astype(F32)
        hidden = x + x * jax.nn.sigmoid(x) * mixed.astype(BF16).astype(F32)
        place = pl.ds(inner % per_chunk * LS, LS)
        hidden_refs[inner // per_chunk][e // per_device, :, place] = hidden.astype(BF16)

    each(LB, first)
    each(LB, second)
    each(LB, third, per_device)


def feature_kernel(
    hidden_ref, above_ref, right_ref, right_back_ref, left_ref, left_back_ref, order_ref,
    out_ref, grad_ref, term_right_ref, term_left_ref, one, two, direct, panel,
):
    @pl.when(pl.program_id(0) == 0)
    def _():
        term_right_ref[...] = jnp.zeros_like(term_right_ref)
        term_left_ref[...] = jnp.zeros_like(term_left_ref)

    def first(b, _):
        one[block_of(b, BS), :] = dot(right_ref[b], hidden_ref[block_of(b, BS), :])

    def second(e, _):
        rows = gathered(one, e, NB, BS)
        panel[e] = rows
        two[block_of(e, BS), :] = dot(left_ref[e], rows)

    def third(e, _):
        rows = block_of(e, BS)
        gate = dot(order_ref[...], gathered(two, e, NB, BS))
        hidden = hidden_ref[rows, :].astype(F32)
        above = above_ref[rows, :].astype(F32)
        sigma = jax.nn.sigmoid(gate)
        through = 1.0 + gate * sigma
        slope = sigma * (1.0 + gate * (1.0 - sigma))
        out_ref[rows, :] = (hidden * through).astype(BF16)
        direct[rows, :] = above * through
        one[rows, :] = above * hidden * slope

    def fourth(e, _):
        rows = gathered_natural(one, e, NB, BS)
        two[block_of(e, BS), :] = dot(left_back_ref[e], rows)
        term_left_ref[e] += dot(panel[e], rows, NT)

    def fifth(b, _):
        rows = gathered(two, b, NB, BS)
        place = block_of(b, BS)
        grad_ref[place, :] = (direct[place, :] + dot(right_back_ref[b], rows)).astype(BF16)
        term_right_ref[b] += dot(hidden_ref[place, :], rows, NT)

    each(NB, first)
    each(NB, second)
    each(NB, third)
    each(NB, fourth)
    each(NB, fifth)


def back_kernel(x_ref, time_ref, first_ref, right_ref, left_back_ref, eye_ref, *refs):
    grad_refs = refs[:CHUNKS]
    out_ref, term_right_ref, term_left_ref, one, two = refs[CHUNKS:]
    devices, _, piece = grad_refs[0].shape
    per_device = LB // devices
    per_chunk = piece // LS

    @pl.when(pl.program_id(0) == 0)
    def _():
        term_right_ref[...] = jnp.zeros_like(term_right_ref)
        term_left_ref[...] = jnp.zeros_like(term_left_ref)

    def grad_of(e, inner):
        place = pl.ds(inner % per_chunk * LS, LS)
        return grad_refs[inner // per_chunk][e // per_device, :, place].astype(F32)

    def first(e, inner):
        x = x_ref[:, block_of(e, LS)].astype(F32)
        grad_time = (grad_of(e, inner) * (x * jax.nn.sigmoid(x))).astype(BF16)
        one[block_of(e, LS), :] = dot(eye_ref[...], grad_time, NT)

    def second(e, _):
        rows = gathered_natural(one, e, LB, LS)
        two[block_of(e, LS), :] = dot(left_back_ref[e], rows)
        term_left_ref[e] += dot(first_ref[e], rows, NT)

    def third(b, inner):
        place = block_of(b, LS)
        rows = gathered(two, b, LB, LS)
        x = x_ref[:, place]
        term = dot(rows, right_ref[b], TN)
        values = x.astype(F32)
        sigma = jax.nn.sigmoid(values)
        slope = sigma * (1.0 + values * (1.0 - sigma))
        grad = grad_of(b, inner)
        result = grad * (1.0 + slope * time_ref[:, place].astype(F32)) + term
        out_ref[:, place] = result.astype(BF16)
        term_right_ref[b] += lax.dot_general(
            x, rows, (((0,), (1,)), ((), ())), preferred_element_type=F32
        )

    each(LB, first, per_device)
    each(LB, second)
    each(LB, third, per_device)


def move(pairs, held, arrive_sems, leave_sems):
    arrive, leave = [], []
    for index, (source, _) in enumerate(pairs):
        arrive.append(pltpu.make_async_copy(source, held.at[index], arrive_sems.at[index]))
        arrive[-1].start()
    for index, (_, target) in enumerate(pairs):
        arrive[index].wait()
        leave.append(pltpu.make_async_copy(held.at[index], target, leave_sems.at[index]))
        leave[-1].start()
    for copy in leave:
        copy.wait()


def places(whole_ref, part, devices, piece):
    return [whole_ref.at[:, pl.ds((d * CHUNKS + part) * piece, piece)] for d in range(devices)]


def split_kernel(part, whole_ref, part_ref, *scratch):
    devices, _, piece = part_ref.shape
    sources = places(whole_ref, part, devices, piece)
    move([(sources[d], part_ref.at[d]) for d in range(devices)], *scratch)


def join_kernel(part, part_ref, *refs):
    whole_ref, scratch = refs[-4], refs[-3:]
    devices, _, piece = part_ref.shape
    targets = places(whole_ref, part, devices, piece)
    move([(part_ref.at[d], targets[d]) for d in range(devices)], *scratch)


def call(kernel, *args, **more):
    return pl.pallas_call(
        kernel, *args, compiler_params=pltpu.CompilerParams(vmem_limit_bytes=VMEM), **more
    )


def fixed(shape):
    return pl.BlockSpec(shape, lambda i: (0,) * len(shape), pipeline_mode=pl.Buffered(1))


def moving(devices, chans, piece):
    return [pltpu.VMEM((devices, chans, piece), BF16)] + [pltpu.SemaphoreType.DMA((devices,))] * 2


def split(whole, devices, part):
    chans, length = whole.shape
    piece = length // (devices * CHUNKS)
    return call(
        functools.partial(split_kernel, part),
        in_specs=[pl.BlockSpec(memory_space=pl.ANY)],
        out_specs=pl.BlockSpec(memory_space=pl.ANY),
        out_shape=jax.ShapeDtypeStruct((devices, chans, piece), whole.dtype),
        scratch_shapes=moving(devices, chans, piece),
        name="split",
    )(whole)


def join(piece_in, part, whole=None):
    devices, chans, piece = piece_in.shape
    args = [piece_in] if whole is None else [piece_in, whole]
    return call(
        functools.partial(join_kernel, part),
        in_specs=[pl.BlockSpec(memory_space=pl.ANY)] * len(args),
        out_specs=pl.BlockSpec(memory_space=pl.ANY),
        out_shape=jax.ShapeDtypeStruct((chans, devices * CHUNKS * piece), piece_in.dtype),
        scratch_shapes=moving(devices, chans, piece),
        input_output_aliases={} if whole is None else {1: 0},
        name="join",
    )(*args)


def mix(inputs, right, left, order, devices):
    chans, length = inputs.shape
    piece = length // (devices * CHUNKS)
    table = fixed((LB, LS, LS))
    strip = pl.BlockSpec((LANES, length), lambda i: (i, 0))
    results = call(
        mix_kernel,
        grid=(chans // LANES,),
        in_specs=[strip, table, table, fixed((LS, LS))],
        out_specs=[pl.BlockSpec((devices, LANES, piece), lambda i: (0, i, 0))] * CHUNKS
        + [strip, pl.BlockSpec((LB, LS, LANES), lambda i: (0, 0, i))],
        out_shape=[jax.ShapeDtypeStruct((devices, chans, piece), BF16)] * CHUNKS
        + [
            jax.ShapeDtypeStruct((chans, length), BF16),
            jax.ShapeDtypeStruct((LB, LS, chans), BF16),
        ],
        scratch_shapes=[pltpu.VMEM((length, LANES), F32)] * 2,
        name="mix",
    )(inputs, right, left, order)
    return results[:CHUNKS], results[CHUNKS], results[CHUNKS + 1]


def feature(hidden, above, right, right_back, left, left_back, order):
    total, piece = hidden.shape
    table = fixed((NB, BS, BS))
    strip = pl.BlockSpec((total, LANES), lambda i: (0, i))
    terms = pl.BlockSpec((NB, BS, BS), lambda i: (0, 0, 0))
    return call(
        feature_kernel,
        grid=(piece // LANES,),
        in_specs=[strip, strip, table, table, table, table, fixed((BS, BS))],
        out_specs=[strip, strip, terms, terms],
        out_shape=[jax.ShapeDtypeStruct((total, piece), BF16)] * 2
        + [jax.ShapeDtypeStruct((NB, BS, BS), F32)] * 2,
        scratch_shapes=[pltpu.VMEM((total, LANES), F32)] * 3
        + [pltpu.VMEM((NB, BS, LANES), BF16)],
        name="feature",
    )(hidden, above, right, right_back, left, left_back, order)


def back(inputs, time_mixed, first_mix, right, left_back, eye, grads):
    chans, length = inputs.shape
    devices, _, piece = grads[0].shape
    table = fixed((LB, LS, LS))
    strip = pl.BlockSpec((LANES, length), lambda i: (i, 0))
    terms = pl.BlockSpec((LB, LS, LS), lambda i: (0, 0, 0))
    return call(
        back_kernel,
        grid=(chans // LANES,),
        in_specs=[
            strip, strip, pl.BlockSpec((LB, LS, LANES), lambda i: (0, 0, i)),
            table, table, fixed((LS, LS)),
        ]
        + [pl.BlockSpec((devices, LANES, piece), lambda i: (0, i, 0))] * CHUNKS,
        out_specs=[strip, terms, terms],
        out_shape=[jax.ShapeDtypeStruct((chans, length), BF16)]
        + [jax.ShapeDtypeStruct((LB, LS, LS), F32)] * 2,
        scratch_shapes=[pltpu.VMEM((length, LANES), F32)] * 2,
        name="back",
    )(inputs, time_mixed, first_mix, right, left_back, eye, *grads)


def unfolded(table, axis, blocks):
    shape = table.shape
    fold = shape[axis] // blocks
    cut = table.reshape(shape[:axis] + (blocks, fold) + shape[axis + 1 :])
    return jnp.swapaxes(cut, axis, axis + 1).reshape(shape)


def folded(table, axis, fold):
    shape = table.shape
    cut = table.reshape(shape[:axis] + (fold, shape[axis] // fold) + shape[axis + 1 :])
    return jnp.swapaxes(cut, axis, axis + 1).reshape(shape)


def log2(size):
    return size.bit_length() - 1


def scatter_sum(terms, groups):
    blocks, size, width = terms[0].shape
    dp, mp = lax.axis_size("dp"), lax.axis_size("mp")

    def halve(parts, name, bit, outer, kind):
        count = lax.axis_size(name)
        mine = (lax.axis_index(name) >> bit) & 1
        parts = [part.reshape(outer, 2, -1, width) for part in parts]
        keep = sum(lax.dynamic_index_in_dim(part, mine, 1, keepdims=False) for part in parts)
        give = sum(lax.dynamic_index_in_dim(part, 1 - mine, 1, keepdims=False) for part in parts)
        got = lax.ppermute(give.astype(kind), name, [(i, i ^ (1 << bit)) for i in range(count)])
        return [keep + got.astype(F32)]

    for bit in range(log2(dp)):
        terms = halve(terms, "dp", bit, blocks * groups * (dp >> (bit + 1)), BF16)
    for bit in range(log2(mp)):
        terms = halve(terms, "mp", bit, mp >> (bit + 1), BF16)
    return terms[0].reshape(blocks // mp, size // dp, width)


def swapped(full, bit):
    mp = lax.axis_size("mp")
    return lax.ppermute(full, "mp", [(i, i ^ (1 << bit)) for i in range(mp)])


def doubled(full, got, bit):
    upper = (lax.axis_index("mp") >> bit) & 1 == 1
    both = jnp.where(upper, jnp.stack([got, full], 1), jnp.stack([full, got], 1))
    return both.reshape((-1,) + full.shape[1:])


def far_tables(*tables):
    share, size, width = tables[0].shape
    dp, mp = lax.axis_size("dp"), lax.axis_size("mp")
    cut = jnp.stack(tables).reshape(len(tables), share, dp, size // dp, width)
    cut = lax.dynamic_index_in_dim(cut, lax.axis_index("dp"), 2, keepdims=False)[None]
    return cut, swapped(cut, log2(mp) - 1)


def column_tables(cut, got):
    top = log2(lax.axis_size("mp")) - 1
    full = doubled(cut, got, top)
    for bit in reversed(range(log2(NEAR), top)):
        full = doubled(full, swapped(full, bit), bit)
    return full


def near_tables(full):
    far = lax.axis_size("mp") // NEAR
    planes = [[z * NEAR + n for n in range(NEAR)] for z in range(far)]
    return lax.all_gather(full, "mp", axis=0, tiled=False, axis_index_groups=planes)


def all_tables(full):
    full = lax.all_gather(full, "dp", axis=0, tiled=False)
    dp, near, far, kinds, share, rows, width = full.shape
    full = full.transpose(3, 2, 1, 4, 0, 5, 6)
    return full.reshape(kinds, near * far * share, dp * rows, width)


def on_device(inputs, cotangent, mixer_right, mixer_left, dense_right, dense_left):
    batch, chans, length = inputs.shape
    devices = lax.axis_size("mp")
    fold = LS // LB
    inputs = inputs.reshape(batch * chans, length)
    cotangent = cotangent.reshape(batch * chans, length)

    def exchange(part):
        shape = part.shape
        part = part.reshape(devices, chans, length // (devices * CHUNKS))
        return lax.all_to_all(part, "mp", 0, 0, tiled=True).reshape(shape)

    def rows(part):
        return part.reshape(devices * chans, -1)

    tables = far_tables(dense_right, dense_left)
    sent = split(cotangent, devices, 0)
    sent, tables, cotangent, inputs, mixer_right, mixer_left = lax.optimization_barrier(
        (sent, tables, cotangent, inputs, mixer_right, mixer_left)
    )
    above = [exchange(sent)]
    tables = column_tables(*tables)

    eye = jnp.eye(LS, dtype=BF16)
    order = unfolded(eye, 0, LB)
    mix_right = unfolded(mixer_right, 2, LB).swapaxes(1, 2)
    mix_left_back = unfolded(unfolded(mixer_left, 1, LB), 2, LB)
    mix_left = mix_left_back.swapaxes(1, 2)
    hidden, time_mixed, first_mix = mix(inputs, mix_right, mix_left, order, devices)
    for part in range(1, CHUNKS):
        sent = split(cotangent, devices, part)
        sent, above[-1], hidden, tables = lax.optimization_barrier(
            (sent, above[-1], hidden, tables)
        )
        above.append(exchange(sent))
    hidden, above, tables = lax.optimization_barrier((hidden, above, near_tables(tables)))
    dense_right, dense_left = all_tables(tables)
    right_back = unfolded(dense_right, 2, NB)
    left_back = unfolded(unfolded(dense_left, 1, NB), 2, NB)
    tables = (right_back.swapaxes(1, 2), right_back, left_back.swapaxes(1, 2), left_back)
    arrived = []
    for part in hidden:
        if arrived:
            part, arrived[-1], tables = lax.optimization_barrier((part, arrived[-1], tables))
        arrived.append(exchange(part))
    outs, grads, rights, lefts = [], [], [], []
    for part in range(CHUNKS):
        out, grad, term_right, term_left = feature(
            rows(arrived[part]), rows(above[part]), *tables, order.T
        )
        outs.append(out.reshape(devices, chans, -1))
        grad = grad.reshape(devices, chans, -1)
        if part:
            grad, grads[-1] = lax.optimization_barrier((grad, grads[-1]))
        grads.append(exchange(grad))
        rights.append(term_right)
        lefts.append(term_left)
    dense_rsum = scatter_sum(rights, 1)
    dense_lsum = scatter_sum(lefts, fold)
    grads, outs, dense_rsum, dense_lsum = lax.optimization_barrier(
        (grads, outs, dense_rsum, dense_lsum)
    )
    returned = [exchange(outs[0])]
    grad_inputs, term_right, term_left = back(
        inputs, time_mixed, first_mix, mix_right, mix_left_back, eye, grads
    )
    grad_inputs, term_right, term_left, outs, returned = lax.optimization_barrier(
        (grad_inputs, term_right, term_left, outs, returned)
    )
    for part in outs[1:]:
        part, returned[-1] = lax.optimization_barrier((part, returned[-1]))
        returned.append(exchange(part))
    mixer_rsum = scatter_sum([term_right], 1)
    mixer_lsum = scatter_sum([term_left], fold)
    block_out = None
    for part in range(CHUNKS):
        block_out = join(returned[part], part, block_out)

    sequences = batch * lax.axis_size("dp")
    dense_scale = float(sequences * length) ** (-0.5)
    mixer_scale = float(sequences * chans * devices) ** (-0.5)
    return (
        block_out.reshape(batch, chans, length),
        grad_inputs.reshape(batch, chans, length),
        folded(mixer_rsum, 2, fold) * mixer_scale,
        folded(folded(mixer_lsum, 1, fold), 2, fold) * mixer_scale,
        folded(dense_rsum, 2, fold) * dense_scale,
        folded(folded(dense_lsum, 1, fold), 2, fold) * dense_scale,
    )


def solution(mesh):
    whole = P("dp", "mp", None)
    table = P("mp", None, None)
    return jax.shard_map(
        on_device,
        mesh=mesh,
        in_specs=(whole, whole, P(), P(), table, table),
        out_specs=(whole, whole) + (P("mp", "dp", None),) * 4,
        check_vma=False,
    )
```
